512 devices in a mesh: dp: 64 (over z_hi, y, core), own: 8 (over z_lo, x).
Axes of the slice: x: 4, y: 8, z: 8 (z_hi: 4, z_lo: 2; z = z_hi * 2 + z_lo), core: 2. Of those that a mesh axis runs over, the one named last changes fastest.
Arguments:
- tokens: bfloat16 [24576, 2048], P('dp'), may hold values from -6 to 6
- norm_gain: float32 [2048], replicated, may hold values from 0.5 to 1.5
- qkv_codes: bfloat16 [2048, 3, 1024], P('dp', None, 'own'), may hold values from -5 to 5
- qkv_scales: float32 [2048, 3, 8], P('dp', None, 'own'), may hold values from 0.011048543 to 0.044194173
- out_codes: bfloat16 [2048, 1024], P('dp', 'own'), may hold values from -5 to 5
- out_scales: float32 [2048, 8], P('dp', 'own'), may hold values from 0.015625 to 0.0625
- block_mask: int32 [192, 9], P('dp'), may hold values from 0 to 1, as said below
- key_counts: int32 [192], replicated, may hold values from 1 to 128, as said below
- upstream: bfloat16 [24576, 2048], P('dp'), may hold values from -0.038085938 to 0.038085938
Outputs:
- mixed: bfloat16 [24576, 2048], P('dp')
- qkv_grad: float32 [2048, 3, 1024], P('dp', None, 'own')
- out_grad: float32 [2048, 1024], P('dp', 'own')
The draws below stay inside these ranges and needn't reach their ends.
Inputs may be any that keep to these rules, and one draw needn't show every extreme that they name: `block_mask`: the entry of a query block's own block is always 1. `key_counts`: some block is full.
All inputs are finite; a program needn't handle non-finite values.
Results may differ from the reference program's by a relative error of at most 0.035.
Values may be sent and summed in bfloat16 or wider, within the bound.
A program may use at most 64 MiB of HBM per device.

```python
import math
import jax
import jax.numpy as jnp
from jax import lax

D = 2048
HEAD = 128
HEADS = 8
BLOCK = 128
TOK_DEV = 384
TOKENS = 24576
HW = 1024
BPD = 3
NQB = 192
KBW = 9
N_DP = 64


def draw_block_mask(key, part):
    first, second = jax.random.split(jax.random.fold_in(key, 11))
    level = jax.random.randint(first, (NQB, 1), 0, 4)
    values = jax.random.randint(second, (NQB, KBW), 0, 4)
    picked = (values <= level).astype(jnp.int32)
    rows = jnp.arange(NQB, dtype=jnp.int32)[:, None]
    columns = jnp.arange(KBW, dtype=jnp.int32)[None, :]
    own_block = columns == BPD + rows % BPD
    return jnp.where(own_block, 1, picked).astype(jnp.int32)


def draw_key_counts(key, part):
    first, second = jax.random.split(jax.random.fold_in(key, 23))
    counts = jax.random.randint(first, (NQB,), 1, BLOCK + 1)
    place = jax.random.randint(second, (), 0, NQB)
    return jnp.where(jnp.arange(NQB, dtype=jnp.int32) == place, BLOCK, counts).astype(jnp.int32)


def block_scale(key, dims, pieces, smallest, high):
    def one(dim, shards_of):
        draws = jax.random.uniform(jax.random.fold_in(jax.random.fold_in(key, 6), dim), (shards_of,), jnp.float32, smallest / len(pieces), high / len(pieces))
        return jnp.repeat(jnp.exp(draws), dims[dim] // shards_of).reshape((-1,) + (1,) * (len(dims) - dim - 1))

    gain = one(*pieces[0])
    for cut in pieces[1:]:
        gain = gain * one(*cut)
    return gain


def centred(stream_key, extent, spread, limit, cuts=(), kind=jnp.bfloat16):
    array = jax.random.normal(stream_key, extent, jnp.float32) * spread
    if len(cuts) > 0:
        array = block_scale(stream_key, extent, cuts, -0.22, 0.18) * array
    return jnp.clip(array, min=-limit, max=limit).astype(kind)


def setup_inputs(seed: int = 0) -> dict:
    keys = jax.random.split(jax.random.key(seed), 10)
    tokens = centred(keys[0], (TOKENS, D), 1.0, 6.0, ((0, 64),))
    norm_gain = jnp.clip(1.0 + 0.1 * jax.random.normal(keys[1], (D,), jnp.float32), 0.5, 1.5)
    qkv_codes = centred(keys[2], (D, 3, HW), 1.0, 5.0, ((0, 64), (2, 8)))
    qkv_scales = jnp.clip(jnp.exp(math.log(0.044194173) - 1.3862944 * jax.random.uniform(keys[3], (D, 3, HEADS), jnp.float32) ** block_scale(keys[3], (D, 3, HEADS), ((0, 64), (2, 8)), -0.2, 0.2)), 0.011048543, 0.044194173)
    out_codes = centred(keys[4], (D, HW), 1.0, 5.0, ((0, 64), (1, 8)))
    out_scales = jnp.clip(jnp.exp(math.log(0.0625) - 1.3862944 * jax.random.uniform(keys[5], (D, HEADS), jnp.float32) ** block_scale(keys[5], (D, HEADS), ((0, 64), (1, 8)), -0.2, 0.2)), 0.015625, 0.0625)
    block_mask = draw_block_mask(jax.random.fold_in(keys[9], 71), 0)
    key_counts = draw_key_counts(jax.random.fold_in(keys[9], 71), 0)
    upstream = centred(keys[8], (TOKENS, D), (TOKENS ** -0.5), 0.038085938, ((0, 64),))
    return {"tokens": tokens, "norm_gain": norm_gain, "qkv_codes": qkv_codes, "qkv_scales": qkv_scales, "out_codes": out_codes, "out_scales": out_scales, "block_mask": block_mask, "key_counts": key_counts, "upstream": upstream}


def attend_range(query_rows, key_rows, value_rows, allowed, datt_rows):
    heads = query_rows.shape[1] // HEAD
    inv_root = 1.0 / HEAD ** 0.5
    query_h = query_rows.astype(jnp.float32).reshape(query_rows.shape[0], heads, HEAD)
    key_h = key_rows.astype(jnp.float32).reshape(key_rows.shape[0], heads, HEAD)
    value_h = value_rows.astype(jnp.float32).reshape(value_rows.shape[0], heads, HEAD)
    datt_h = datt_rows.astype(jnp.float32).reshape(datt_rows.shape[0], heads, HEAD)
    scores = jnp.einsum('qhe,khe->hqk', query_h, key_h) * inv_root
    expo = jnp.where(allowed[None], jnp.exp(jnp.where(allowed[None], scores, 0.0)), 0.0)
    probs = expo / lax.optimization_barrier(jnp.sum(expo, axis=-1, keepdims=True))
    probs_b = probs.astype(jnp.bfloat16).astype(jnp.float32)
    attended = jnp.einsum('hqk,khe->qhe', probs_b, value_h).astype(jnp.bfloat16)
    d_prob = jnp.einsum('qhe,khe->hqk', datt_h, value_h)
    delta = lax.optimization_barrier(jnp.sum(probs * d_prob, axis=-1, keepdims=True))
    d_score = (probs * (d_prob - delta) * inv_root).astype(jnp.bfloat16).astype(jnp.float32)
    grad_query = jnp.einsum('hqk,khe->qhe', d_score, key_h).astype(jnp.bfloat16)
    grad_key = jnp.einsum('hqk,qhe->khe', d_score, query_h)
    grad_value = jnp.einsum('hqk,qhe->khe', probs_b, datt_h)
    rows = query_rows.shape[0]
    width = query_rows.shape[1]
    return (attended.reshape(rows, width), grad_query.reshape(rows, width), grad_key.reshape(-1, width), grad_value.reshape(-1, width))

def reference(tokens, norm_gain, qkv_codes, qkv_scales, out_codes, out_scales, block_mask, key_counts, upstream):
    xfloat = tokens.astype(jnp.float32)
    factor = lax.rsqrt(lax.optimization_barrier(jnp.mean(xfloat * xfloat, axis=-1, keepdims=True)) + 1e-05)
    normed = (xfloat * factor * norm_gain[None, :]).astype(jnp.bfloat16)
    w_qkv = (qkv_codes.astype(jnp.float32).reshape(D, 3, HEADS, HEAD) * qkv_scales[..., None]).reshape(D, 3 * HW).astype(jnp.bfloat16)
    w_out = (out_codes.astype(jnp.float32).reshape(D, HEADS, HEAD) * out_scales[..., None]).reshape(D, HW).astype(jnp.bfloat16)
    qkv = jnp.dot(normed, w_qkv, preferred_element_type=jnp.float32).astype(jnp.bfloat16).reshape(TOKENS, 3, HW)
    queries = qkv[:, 0]
    zero_pad = jnp.zeros((TOK_DEV, HW), jnp.bfloat16)
    keys_pad = jnp.concatenate([zero_pad, qkv[:, 1], zero_pad], axis=0)
    values_pad = jnp.concatenate([zero_pad, qkv[:, 2], zero_pad], axis=0)
    counts_pad = jnp.concatenate([jnp.zeros((BPD,), jnp.int32), key_counts, jnp.zeros((BPD,), jnp.int32)])
    d_att = jnp.dot(upstream, w_out, preferred_element_type=jnp.float32).astype(jnp.bfloat16)
    within = jnp.arange(KBW * BLOCK, dtype=jnp.int32) % BLOCK

    def one_range(index):
        index = index.astype(jnp.int32)
        start = (index * TOK_DEV).astype(jnp.int32)
        query_rows = lax.dynamic_slice_in_dim(queries, start, TOK_DEV, 0)
        key_rows = lax.dynamic_slice_in_dim(keys_pad, start, 3 * TOK_DEV, 0)
        value_rows = lax.dynamic_slice_in_dim(values_pad, start, 3 * TOK_DEV, 0)
        datt_rows = lax.dynamic_slice_in_dim(d_att, start, TOK_DEV, 0)
        mask_rows = lax.dynamic_slice_in_dim(block_mask, (index * BPD).astype(jnp.int32), BPD, 0)
        counts_win = lax.dynamic_slice_in_dim(counts_pad, (index * BPD).astype(jnp.int32), KBW, 0)
        live = within < jnp.repeat(counts_win, BLOCK)
        blocks = jnp.repeat(jnp.repeat(mask_rows, BLOCK, axis=0), BLOCK, axis=1) > 0
        allowed = jnp.logical_and(blocks, live[None, :])
        return attend_range(query_rows, key_rows, value_rows, allowed, datt_rows)
    attended, grad_query, grad_key, grad_value = lax.map(one_range, jnp.arange(N_DP, dtype=jnp.int32))
    attended = attended.reshape(TOKENS, HW)
    grad_query = grad_query.reshape(TOKENS, HW)

    def fold_back(parts):
        parts = parts.reshape(N_DP, 3, TOK_DEV, HW)
        zero_one = jnp.zeros((1, TOK_DEV, HW), jnp.float32)
        from_next = jnp.concatenate([parts[1:, 0], zero_one], axis=0)
        from_prev = jnp.concatenate([zero_one, parts[:-1, 2]], axis=0)
        return (parts[:, 1] + from_next + from_prev).astype(jnp.bfloat16).reshape(TOKENS, HW)
    grad_key = fold_back(grad_key)
    grad_value = fold_back(grad_value)
    mixed = jnp.dot(attended, w_out.T, preferred_element_type=jnp.float32).astype(jnp.bfloat16)
    out_grad = jnp.dot(upstream.T, attended, preferred_element_type=jnp.float32)
    d_qkv = jnp.stack([grad_query, grad_key, grad_value], axis=1).reshape(TOKENS, 3 * HW)
    qkv_grad = jnp.dot(normed.T, d_qkv, preferred_element_type=jnp.float32).reshape(D, 3, HW)
    return (mixed, qkv_grad, out_grad)
```

```python
import functools
import math

import jax
import jax.numpy as jnp
from jax import lax
from jax.experimental import pallas as pl
from jax.experimental.pallas import tpu as pltpu
from jax.sharding import Mesh
from jax.sharding import PartitionSpec as P

HEAD = 128
BLK = 128
ROWS = 32
COLS = 4 * HEAD
AXES = ("zh", "y", "core", "zl", "x")
DP = ("zh", "y", "core")
OWN = ("zl", "x")
BF = jnp.bfloat16
F32 = jnp.float32
MESH = pl.DeviceIdType.MESH
INV_ROOT = 1.0 / HEAD**0.5
TO_EXP2 = INV_ROOT * math.log2(math.e)


def nn(a, b):
    return lax.dot_general(a, b, (((1,), (0,)), ((), ())), preferred_element_type=F32)


def nt(a, b):
    return lax.dot_general(a, b, (((1,), (1,)), ((), ())), preferred_element_type=F32)


def tn(a, b):
    return lax.dot_general(a, b, (((0,), (0,)), ((), ())), preferred_element_type=F32)


def kernel(
    dims,
    tok, gain, wblk, bias, ups,
    mixed, gq, go,
    normed, ntr, utr, nts, uts, wbuf, qd, kv, ebuf, pbuf, dsb, dqa, atts, att_all, wo, mxs,
    hgs, hgr, ogr, dd, g, rss, rsr, zs, zr,
    agz, agy, ags, halo, tsw, wos, ats, hgm, dds, rsm, zsm, mxm, loc,
):
    ZH, Y, ZL, X = dims
    H = Y // 2
    NOWN = ZL * X
    T, D = tok.shape
    NQ = T // BLK
    share = D // NOWN
    ny = ZH * Y // NOWN
    zh, y, c = lax.axis_index("zh"), lax.axis_index("y"), lax.axis_index("core")
    own = lax.axis_index("zl") * X + lax.axis_index("x")
    sib = {"core": 1 - c}
    pending = []

    def rcopy(src, dst, sems, index, dev):
        return pltpu.make_async_remote_copy(
            src_ref=src,
            dst_ref=dst,
            send_sem=sems.at[(0, *index)],
            recv_sem=sems.at[(1, *index)],
            device_id=dev,
            device_id_type=MESH,
        )

    def send(src, dst, sems, index, dev):
        cp = rcopy(src, dst, sems, index, dev)
        cp.start()
        pending.append(cp)

    def arrived(dst, sems, index, dev):
        rcopy(dst, dst, sems, index, dev).wait_recv()

    def zk(k):
        return lax.rem(zh + k, ZH)

    def yd(d):
        return lax.rem(y + (d + Y), Y)

    def ydev(d):
        return {"y": yd(d)}

    def owner(j):
        return lax.rem(own + j, NOWN)

    def odev(o):
        return {"zl": o // X, "x": lax.rem(o, X)}

    def half(d, k):
        return (k < ZH // 2) == (d == 0)

    place = (zh * Y + y) * 2 + c
    count = ZH * Y * 2

    def range_dev(step):
        r = lax.rem(place + step + count, count)
        return {"zh": r // (2 * Y), "y": lax.rem(r // 2, Y), "core": lax.rem(r, 2)}

    nxt, prv = range_dev(1), range_dev(-1)

    barrier = pltpu.get_barrier_semaphore()
    partners = [sib, ydev(1), ydev(-1), nxt, prv]
    partners += [{"zh": zk(k)} for k in range(1, ZH)]
    partners += [odev(owner(j)) for j in range(1, NOWN)]
    for dev in partners:
        pl.semaphore_signal(barrier, inc=1, device_id=dev, device_id_type=MESH)
    wbuf[zh, y, c] = wblk[...]
    pl.semaphore_wait(barrier, len(partners))

    def block(k, d):
        return wbuf.at[zk(k), yd(d), c]

    def ag_send(d, h, k):
        s = 1 if d == 0 else -1
        b = block(k, -s * (h - 1))
        send(b, b, agy, (d, h - 1, k), ydev(s))

    def ag_wait(d, h, k):
        s = 1 if d == 0 else -1
        arrived(block(k, -s * h), agy, (d, h - 1, k), ydev(s))

    def ag_pass(dy):
        b = wbuf.at[:, yd(dy), c]
        send(b, b, ags, (dy % Y,), sib)

    mine = wbuf.at[zh, y, c]
    ag_send(0, 1, 0)
    ag_send(1, 1, 0)
    for k in range(1, ZH):
        send(mine, mine, agz, (k,), {"zh": zk(k)})

    def norm_rows(i, carry):
        r = pl.ds(pl.multiple_of(i * 16, 16), 16)
        x = tok[r, :].astype(F32)
        factor = lax.rsqrt(jnp.mean(x * x, axis=-1, keepdims=True) + 1e-05)
        normed[r, :] = (x * factor * gain[...]).astype(BF)
        return carry

    def turn(src, dst):
        per = Y // 2

        def body(j, carry):
            v = src[:, pl.ds(pl.multiple_of(j * 128, 128), 128)]
            dst[j // per, pl.ds(2 * lax.rem(j, per), 2)] = v.T.reshape(2, 2, ROWS, T)
            return carry

        return body

    lax.fori_loop(0, T // 16, norm_rows, 0)
    for k in range(1, ZH):
        arrived(wbuf.at[zk(ZH - k), y, c], agz, (k,), sib)
    for k in range(1, ZH):
        ag_send(0, 1, k)
        ag_send(1, 1, k)
    ag_pass(0)

    def fill(h):
        if h == 1:
            lax.fori_loop(0, D // 128, turn(ups, utr), 0)
            send(utr.at[:, :, 1 - c], uts, tsw, (0,), sib)
        if h == 2:
            lax.fori_loop(0, D // 128, turn(normed, ntr), 0)
            send(ntr.at[:, :, 1 - c], nts, tsw, (1,), sib)

    for h in range(1, H + 1):
        for k in range(ZH):
            for d in (0, 1):
                if h == H and not half(d, k):
                    continue
                ag_wait(d, h, k)
                if h < H - 1 or (h == H - 1 and half(d, k)):
                    ag_send(d, h + 1, k)
        ag_pass(-h)
        if h < H:
            ag_pass(h)
        fill(h)
    for dy in range(Y):
        arrived(wbuf.at[:, yd(dy), 1 - c], ags, (dy,), sib)

    def project(src, lo, n):
        total = None
        for z in range(ZH):
            w = wbuf[z, :, :, :, lo : lo + n].reshape(Y * 2 * ROWS, n)
            term = nn(src[:, z * Y * 64 : (z + 1) * Y * 64], w)
            total = term if total is None else total + term
        return total.astype(BF)

    keyval = project(normed, HEAD, 2 * HEAD)
    kv[1, 0] = keyval[:, :HEAD]
    kv[1, 1] = keyval[:, HEAD:]
    for j in range(2):
        send(kv.at[1, j], kv.at[0, j], halo, (0, j), nxt)
        send(kv.at[1, j], kv.at[2, j], halo, (1, j), prv)
    qd[0] = project(normed, 0, HEAD)
    qd[1] = project(ups, 3 * HEAD, HEAD)

    def wo_part(o):
        at = o * ny
        return wbuf.at[at // Y, pl.ds(lax.rem(at, Y), ny), :, :, pl.ds(3 * HEAD, HEAD)]

    def lanes(o, n):
        return pl.ds(pl.multiple_of(o * n, n), n)

    for j in range(1, NOWN):
        o = owner(j)
        send(wo_part(o), wo.at[:, :, :, lanes(own, HEAD)], wos, (j,), odev(o))
    keep_wo = pltpu.make_async_copy(wo_part(own), wo.at[:, :, :, lanes(own, HEAD)], loc.at[0])
    keep_wo.start()

    sums = [None] * NQ
    for seg in (1, 0, 2):
        if seg != 1:
            arrived(kv.at[seg, 0], halo, (seg // 2, 0), sib)
        for b in range(NQ):
            rows = slice(b * BLK, (b + 1) * BLK)
            score = nt(qd[0, rows, :], kv[seg, 0])
            e = jnp.exp2(score * TO_EXP2 + bias[b * 3 + seg : b * 3 + seg + 1, :])
            ebuf[seg, rows, :] = e
            part = jnp.sum(e, axis=-1, keepdims=True)
            sums[b] = part if sums[b] is None else sums[b] + part
    for seg in (0, 2):
        arrived(kv.at[seg, 1], halo, (seg // 2, 1), sib)
    deltas = []
    for b in range(NQ):
        rows = slice(b * BLK, (b + 1) * BLK)
        scale = 1.0 / sums[b]
        total = None
        for seg in range(3):
            p = ebuf[seg, rows, :] * scale
            ebuf[seg, rows, :] = p
            pb = p.astype(BF)
            pbuf[seg, rows, :] = pb
            term = nn(pb, kv[seg, 1])
            total = term if total is None else total + term
        atts[rows, :] = total.astype(BF)
        deltas.append(jnp.sum(total * qd[1, rows, :].astype(F32), axis=-1, keepdims=True))
    for j in range(1, NOWN):
        o = owner(j)
        send(atts, att_all.at[:, lanes(own, HEAD)], ats, (j,), odev(o))
    keep_att = pltpu.make_async_copy(atts, att_all.at[:, lanes(own, HEAD)], loc.at[1])
    keep_att.start()
    dd[0, :, 3 * HEAD :] = atts[...]
    send(dd.at[0, :, pl.ds(3 * HEAD, HEAD)], dd.at[1, :, pl.ds(3 * HEAD, HEAD)], dds, (0,), sib)

    for seg in (0, 2, 1):
        for b in range(NQ):
            rows = slice(b * BLK, (b + 1) * BLK)
            dp = nt(qd[1, rows, :], kv[seg, 1])
            ds = (ebuf[seg, rows, :] * (dp - deltas[b]) * INV_ROOT).astype(BF)
            dsb[seg, rows, :] = ds
            term = nn(ds, kv[seg, 0])
            if seg == 0:
                dqa[rows, :] = term
            else:
                dqa[rows, :] += term
        dk = tn(dsb[seg], qd[0])
        dv = tn(pbuf[seg], qd[1])
        if seg == 1:
            ogr[0] = dk
            ogr[1] = dv
        else:
            hgs[seg // 2, 0] = dk.astype(BF)
            hgs[seg // 2, 1] = dv.astype(BF)
            send(hgs.at[seg // 2], hgr.at[seg // 2], hgm, (seg // 2,), prv if seg == 0 else nxt)
    dd[0, :, :HEAD] = dqa[...].astype(BF)
    for side in range(2):
        arrived(hgr.at[side], hgm, (side,), sib)
    for j in range(2):
        both = ogr[j] + hgr[0, j].astype(F32) + hgr[1, j].astype(F32)
        dd[0, :, (j + 1) * HEAD : (j + 2) * HEAD] = both.astype(BF)
    send(dd.at[0, :, pl.ds(0, 3 * HEAD)], dd.at[1, :, pl.ds(0, 3 * HEAD)], dds, (1,), sib)
    arrived(uts, tsw, (0,), sib)
    arrived(nts, tsw, (1,), sib)
    arrived(dd.at[1, :, pl.ds(3 * HEAD, HEAD)], dds, (0,), sib)
    arrived(dd.at[1, :, pl.ds(0, 3 * HEAD)], dds, (1,), sib)

    def term_at(dy):
        yy = yd(dy)
        high = ZH * ROWS
        a = nn(ntr[:, yy, c].reshape(high, T), dd[0, :, : 3 * HEAD])
        a += nn(nts[:, yy].reshape(high, T), dd[1, :, : 3 * HEAD])
        b = nn(utr[:, yy, c].reshape(high, T), dd[0, :, 3 * HEAD :])
        b += nn(uts[:, yy].reshape(high, T), dd[1, :, 3 * HEAD :])
        g[dy % Y, :, :, : 3 * HEAD] = a.reshape(ZH, ROWS, 3 * HEAD)
        g[dy % Y, :, :, 3 * HEAD :] = b.reshape(ZH, ROWS, HEAD)

    def rs_wait(d, t, k):
        arrived(rsr.at[d, t, k], rsm, (d, t, k), sib)

    def mix():
        keep_wo.wait()
        keep_att.wait()
        for j in range(1, NOWN):
            o = owner(NOWN - j)
            arrived(wo.at[:, :, :, lanes(o, HEAD)], wos, (j,), sib)
            arrived(att_all.at[:, lanes(o, HEAD)], ats, (j,), sib)
        w = wo[...].reshape(share, NOWN * HEAD)
        for b in range(NQ):
            rows = slice(b * BLK, (b + 1) * BLK)
            mxs[rows, :] = nt(att_all[rows, :], w).astype(BF)
        for j in range(1, NOWN):
            send(mxs, mixed.at[:, lanes(own, share)], mxm, (j,), odev(owner(j)))

    order = [*range(1, ZH), 0]
    for t in range(H):
        term_at(H - t)
        if t > 0:
            term_at(t - H)
        if t == H - 1:
            term_at(0)
        for k in order:
            for d in (0, 1):
                s = 1 if d == 0 else -1
                if t == 0 and not half(d, k):
                    continue
                val = g[(s * (H - t)) % Y, zk(k)]
                if t > 1 or (t == 1 and half(d, k)):
                    rs_wait(d, t - 1, k)
                    val += rsr[d, t - 1, k].astype(F32)
                rss[d, t, k] = val.astype(BF)
                send(rss.at[d, t, k], rsr.at[d, t, k], rsm, (d, t, k), ydev(s))
        if t == 1:
            mix()
    kept = None
    for k in order:
        val = g[0, zk(k)]
        for d in (0, 1):
            rs_wait(d, H - 1, k)
            val += rsr[d, H - 1, k].astype(F32)
        if k:
            zs[k] = val.astype(BF)
            send(zs.at[k], zr.at[k], zsm, (k,), {"zh": zk(k)})
        else:
            kept = val
    for k in range(1, ZH):
        arrived(zr.at[k], zsm, (k,), sib)
        kept += zr[k].astype(F32)
    gq[...] = kept[:, : 3 * HEAD]
    go[...] = kept[:, 3 * HEAD :]

    keep_mix = pltpu.make_async_copy(mxs, mixed.at[:, lanes(own, share)], loc.at[2])
    keep_mix.start()
    keep_mix.wait()
    for j in range(1, NOWN):
        arrived(mixed.at[:, lanes(owner(NOWN - j), share)], mxm, (j,), sib)
    for cp in pending:
        cp.wait_send()


def per_device(
    dims,
    tokens, norm_gain, qkv_codes, qkv_scales, out_codes, out_scales, block_mask, key_counts, upstream,
):
    ZH, Y, ZL, X = dims
    H = Y // 2
    NOWN = ZL * X
    T, D = tokens.shape
    place = lax.axis_index(DP)
    blocks = block_mask.shape[0]
    window = block_mask.shape[1]
    w_qkv = (qkv_codes.astype(F32) * qkv_scales).reshape(ROWS, 3 * HEAD)
    w_out = out_codes.astype(F32) * out_scales
    wblk = jnp.concatenate([w_qkv, w_out], axis=1).astype(BF)
    pad = jnp.zeros((blocks,), jnp.int32)
    counts = lax.dynamic_slice_in_dim(
        jnp.concatenate([pad, key_counts, pad]), place * blocks, window, 0
    )
    within = jnp.arange(BLK, dtype=jnp.int32)
    live = within[None, :] < counts[:, None]
    allowed = jnp.logical_and(block_mask[:, :, None] > 0, live[None])
    bias = jnp.where(allowed, 0.0, -1e30).astype(F32).reshape(blocks * 3, T)

    vmem = pl.BlockSpec(memory_space=pltpu.VMEM)
    buffers = [
        ((T, D), BF),
        ((ZH, Y, 2, ROWS, T), BF),
        ((ZH, Y, 2, ROWS, T), BF),
        ((ZH, Y, ROWS, T), BF),
        ((ZH, Y, ROWS, T), BF),
        ((ZH, Y, 2, ROWS, COLS), BF),
        ((2, T, HEAD), BF),
        ((3, 2, T, HEAD), BF),
        ((3, T, T), F32),
        ((3, T, T), BF),
        ((3, T, T), BF),
        ((T, HEAD), F32),
        ((T, HEAD), BF),
        ((T, NOWN * HEAD), BF),
        ((ZH * Y // NOWN, 2, ROWS, NOWN * HEAD), BF),
        ((T, D // NOWN), BF),
        ((2, 2, T, HEAD), BF),
        ((2, 2, T, HEAD), BF),
        ((2, T, HEAD), F32),
        ((2, T, COLS), BF),
        ((Y, ZH, ROWS, COLS), F32),
        ((2, H, ZH, ROWS, COLS), BF),
        ((2, H, ZH, ROWS, COLS), BF),
        ((ZH, ROWS, COLS), BF),
        ((ZH, ROWS, COLS), BF),
    ]
    sems = [
        (2, ZH), (2, 2, H, ZH), (2, Y), (2, 2, 2), (2, 2), (2, NOWN), (2, NOWN), (2, 2), (2, 2),
        (2, 2, H, ZH), (2, ZH), (2, NOWN), (3,),
    ]
    mixed, gq, go = pl.pallas_call(
        functools.partial(kernel, dims),
        out_shape=(
            jax.ShapeDtypeStruct((T, D), BF),
            jax.ShapeDtypeStruct((ROWS, 3 * HEAD), F32),
            jax.ShapeDtypeStruct((ROWS, HEAD), F32),
        ),
        in_specs=[vmem] * 5,
        out_specs=(vmem,) * 3,
        scratch_shapes=[pltpu.VMEM(s, t) for s, t in buffers]
        + [pltpu.SemaphoreType.DMA(s) for s in sems],
        compiler_params=pltpu.CompilerParams(
            collective_id=0, has_side_effects=True, vmem_limit_bytes=50 * 1024 * 1024
        ),
        cost_estimate=pl.CostEstimate(
            flops=2_600_000_000, bytes_accessed=6_000_000, transcendentals=500_000
        ),
    )(tokens, norm_gain.reshape(1, D), wblk, bias, upstream)
    return mixed, gq.reshape(ROWS, 3, HEAD), go


def build(torus):
    s = torus.shape
    dims = (s["zh"], s["y"], s["zl"], s["x"])
    placed = (
        P(DP, None), P(), P(DP, None, OWN), P(DP, None, OWN), P(DP, OWN), P(DP, OWN), P(DP, None),
        P(), P(DP, None),
    )
    return jax.shard_map(
        functools.partial(per_device, dims),
        mesh=torus,
        in_specs=placed,
        out_specs=(P(DP, None), P(DP, None, OWN), P(DP, OWN)),
        check_vma=False,
    )


def solution(mesh):
    return build(Mesh(mesh.devices.reshape(4, 8, 2, 2, 4), AXES))
```

```python
import functools
import math

import jax
import jax.numpy as jnp
from jax import lax
from jax.experimental import pallas as pl
from jax.experimental.pallas import tpu as pltpu
from jax.sharding import Mesh
from jax.sharding import PartitionSpec as P

HEAD = 128
BLK = 128
ROWS = 32
COLS = 4 * HEAD
AXES = ("zh", "y", "core", "zl", "x")
DP = ("zh", "y", "core")
OWN = ("zl", "x")
BF = jnp.bfloat16
F32 = jnp.float32
MESH = pl.DeviceIdType.MESH
INV_ROOT = 1.0 / HEAD**0.5
TO_EXP2 = INV_ROOT * math.log2(math.e)


def nn(a, b):
    return lax.dot_general(a, b, (((1,), (0,)), ((), ())), preferred_element_type=F32)


def nt(a, b):
    return lax.dot_general(a, b, (((1,), (1,)), ((), ())), preferred_element_type=F32)


def tn(a, b):
    return lax.dot_general(a, b, (((0,), (0,)), ((), ())), preferred_element_type=F32)


def kernel(
    dims,
    tok_hbm, gain, codes, scales, ocodes, oscales, maskb, counts, ups_hbm,
    mixed, gq, go,
    tok, ups, bias, normed, ntr, utr, nts, uts, wbuf, wof, qd, kv, ebuf, pbuf, dsb, dqa, atts,
    att_all, hgs, hgr, ogr, dd, g, rss, rsr, fin, zs, zr,
    agz, agy, ags, halo, tsw, wos, wps, ats, hgm, dds, rsm, zsm, loc,
):
    ZH, Y, ZL, X = dims
    H = Y // 2
    ZP = ZH // 2
    W = 2 * HEAD
    NOWN = ZL * X
    T, D = tok.shape
    NQ = T // BLK
    SEG = T // BLK
    zh, y, c = lax.axis_index("zh"), lax.axis_index("y"), lax.axis_index("core")
    own = lax.axis_index("zl") * X + lax.axis_index("x")
    sib = {"core": 1 - c}
    pending = {}
    locals_ = []

    def rcopy(src, dst, sems, index, dev):
        return pltpu.make_async_remote_copy(
            src_ref=src,
            dst_ref=dst,
            send_sem=sems.at[(0, *index)],
            recv_sem=sems.at[(1, *index)],
            device_id=dev,
            device_id_type=MESH,
        )

    def send(src, dst, sems, index, dev):
        cp = rcopy(src, dst, sems, index, dev)
        cp.start()
        pending[id(sems), index] = [cp, True]

    def arrived(dst, sems, index):
        rcopy(dst, dst, sems, index, sib).wait_recv()
        pending[id(sems), index][1] = False

    def finish():
        for cp in locals_:
            cp.wait()
        for cp, due in pending.values():
            if due:
                cp.wait_recv()
            cp.wait_send()

    def keep(src, dst, i):
        cp = pltpu.make_async_copy(src, dst, loc.at[i])
        cp.start()
        return cp

    def zk(k):
        return lax.rem(zh + k, ZH)

    def yd(d):
        return lax.rem(y + (d + Y), Y)

    def ydev(d):
        return {"y": yd(d)}

    def owner(j):
        return lax.rem(own + j, NOWN)

    def odev(o):
        return {"zl": o // X, "x": lax.rem(o, X)}

    def lanes(o, n):
        return pl.ds(pl.multiple_of(o * n, n), n)

    place = (zh * Y + y) * 2 + c
    count = ZH * Y * 2

    def range_dev(step):
        r = lax.rem(place + step + count, count)
        return {"zh": r // (2 * Y), "y": lax.rem(r // 2, Y), "core": lax.rem(r, 2)}

    nxt, prv = range_dev(1), range_dev(-1)

    barrier = pltpu.get_barrier_semaphore()
    partners = [odev(owner(j)) for j in range(1, NOWN)]
    partners += [{"zh": zk(k)} for k in range(1, ZH)]
    partners += [nxt, prv, ydev(1), ydev(-1), sib]
    for dev in partners:
        pl.semaphore_signal(barrier, inc=1, device_id=dev, device_id_type=MESH)
    load_tok = keep(tok_hbm, tok, 0)
    load_ups = keep(ups_hbm, ups, 1)

    eye = lax.broadcasted_iota(jnp.int32, (ROWS, ROWS), 0) == lax.broadcasted_iota(
        jnp.int32, (ROWS, ROWS), 1
    )

    def column(row):
        return jnp.sum(jnp.where(eye, row, 0.0), axis=1, keepdims=True)

    for at, j in enumerate((1, 2, 0)):
        part = codes[j].astype(F32) * column(scales[j])
        wbuf[zh, y, c, :, at * HEAD : (at + 1) * HEAD] = part.astype(BF)
    part = ocodes[...].astype(F32) * column(oscales[...])
    wbuf[zh, y, c, :, 3 * HEAD :] = part.astype(BF)

    blocks = lax.broadcasted_iota(jnp.int32, counts.shape, 1)
    within = lax.broadcasted_iota(jnp.int32, (1, BLK), 1)
    for j in range(3 * SEG):
        which = place * SEG + (j - SEG)
        alive = jnp.sum(jnp.where(blocks == which, counts[...], 0), axis=1, keepdims=True)
        for b in range(NQ):
            ok = jnp.logical_and(within < alive, maskb[b : b + 1, j : j + 1] > 0)
            row = b * 3 + j // SEG
            lo = (j % SEG) * BLK
            bias[row : row + 1, lo : lo + BLK] = jnp.where(ok, 0.0, -1e30)
    pl.semaphore_wait(barrier, len(partners))

    def cols(h):
        return pl.ds(h * W, W)

    def piece(h, q, d):
        return wbuf.at[pl.ds(q * ZP, ZP), yd(d), c, :, cols(h)]

    def ag_send(d, t, h, q):
        s = 1 if d == 0 else -1
        b = piece(h, q, -s * (t - 1))
        send(b, b, agy, (d, t - 1, h, q), ydev(s))

    def ag_wait(d, t, h, q):
        s = 1 if d == 0 else -1
        arrived(piece(h, q, -s * t), agy, (d, t - 1, h, q))

    def ag_pass(h, dy):
        b = wbuf.at[:, yd(dy), c, :, cols(h)]
        send(b, b, ags, (h, dy % Y), sib)

    def wof_send(dy):
        src = wbuf.at[:, yd(dy), c, :, pl.ds(3 * HEAD, HEAD)]
        for j in range(1, NOWN):
            o = owner(j)
            rcopy(src, wof.at[:, yd(dy), c, :, lanes(own, HEAD)], wos, (j,), odev(o)).start()

    def ag_z(h):
        for k in range(1, ZH):
            arrived(wbuf.at[zk(ZH - k), y, c, :, cols(h)], agz, (h, k))
        for q in range(2):
            for d in range(2):
                ag_send(d, 1, h, q)
        ag_pass(h, 0)

    for h in range(2):
        mine = wbuf.at[zh, y, c, :, cols(h)]
        for k in (2, 1, 3)[: ZH - 1] if ZH == 4 else range(1, ZH):
            send(mine, mine, agz, (h, k), {"zh": zk(k)})

    def norm_rows(i, carry):
        r = pl.ds(pl.multiple_of(i * 16, 16), 16)
        x = tok[r, :].astype(F32)
        factor = lax.rsqrt(jnp.mean(x * x, axis=-1, keepdims=True) + 1e-05)
        normed[r, :] = (x * factor * gain[...]).astype(BF)
        return carry

    def turn(src, dst):
        per = Y // 2

        def body(j, carry):
            v = src[:, pl.ds(pl.multiple_of(j * 128, 128), 128)]
            dst[j // per, pl.ds(2 * lax.rem(j, per), 2)] = v.T.reshape(2, 2, ROWS, T)
            return carry

        return body

    load_tok.wait()
    lax.fori_loop(0, T // 16, norm_rows, 0)
    ag_z(0)
    ag_z(1)
    wof_send(0)
    load_ups.wait()

    def fill(t):
        if t == 1:
            lax.fori_loop(0, D // 128, turn(ups, utr), 0)
            send(utr.at[:, :, 1 - c], uts, tsw, (0,), sib)
        if t == 2:
            lax.fori_loop(0, D // 128, turn(normed, ntr), 0)
            send(ntr.at[:, :, 1 - c], nts, tsw, (1,), sib)

    for t in range(1, H + 1):
        for h in range(2):
            for q in range(2):
                for d in range(2):
                    if t == H and q != d:
                        continue
                    ag_wait(d, t, h, q)
                    if t < H - 1 or (t == H - 1 and q == d):
                        ag_send(d, t + 1, h, q)
            ag_pass(h, -t)
            if t < H:
                ag_pass(h, t)
        wof_send(-t)
        if t < H:
            wof_send(t)
        fill(t)

    def from_sibling(h):
        for dy in range(Y):
            arrived(wbuf.at[:, yd(dy), 1 - c, :, cols(h)], ags, (h, dy))

    def project(src, lo, n):
        total = None
        for z in range(ZH):
            w = wbuf[z, :, :, :, lo : lo + n].reshape(Y * 2 * ROWS, n)
            term = nn(src[:, z * Y * 64 : (z + 1) * Y * 64], w)
            total = term if total is None else total + term
        return total.astype(BF)

    from_sibling(0)
    keyval = project(normed, 0, W)
    kv[1, 0] = keyval[:, :HEAD]
    kv[1, 1] = keyval[:, HEAD:]
    for j in range(2):
        send(kv.at[1, j], kv.at[0, j], halo, (0, j), nxt)
        send(kv.at[1, j], kv.at[2, j], halo, (1, j), prv)
    from_sibling(1)
    qd[0] = project(normed, W, HEAD)
    qd[1] = project(ups, 3 * HEAD, HEAD)
    keep_wo = keep(
        wbuf.at[:, :, :, :, pl.ds(3 * HEAD, HEAD)], wof.at[:, :, :, :, lanes(own, HEAD)], 2
    )

    sums = [None] * NQ
    for seg in (1, 0, 2):
        if seg != 1:
            arrived(kv.at[seg, 0], halo, (seg // 2, 0))
        for b in range(NQ):
            rows = slice(b * BLK, (b + 1) * BLK)
            score = nt(qd[0, rows, :], kv[seg, 0])
            e = jnp.exp2(score * TO_EXP2 + bias[b * 3 + seg : b * 3 + seg + 1, :])
            ebuf[seg, rows, :] = e
            part = jnp.sum(e, axis=-1, keepdims=True)
            sums[b] = part if sums[b] is None else sums[b] + part
    for seg in (0, 2):
        arrived(kv.at[seg, 1], halo, (seg // 2, 1))
    deltas = []
    for b in range(NQ):
        rows = slice(b * BLK, (b + 1) * BLK)
        scale = 1.0 / sums[b]
        total = None
        for seg in range(3):
            p = ebuf[seg, rows, :] * scale
            ebuf[seg, rows, :] = p
            pb = p.astype(BF)
            pbuf[seg, rows, :] = pb
            term = nn(pb, kv[seg, 1])
            total = term if total is None else total + term
        atts[rows, :] = total.astype(BF)
        deltas.append(jnp.sum(total * qd[1, rows, :].astype(F32), axis=-1, keepdims=True))
    dd[0, :, 3 * HEAD :] = atts[...]
    send(dd.at[0, :, pl.ds(3 * HEAD, HEAD)], dd.at[1, :, pl.ds(3 * HEAD, HEAD)], dds, (0,), sib)
    for j in range(1, NOWN):
        send(atts, att_all.at[:, lanes(own, HEAD)], ats, (j,), odev(owner(j)))
    keep_att = keep(atts, att_all.at[:, lanes(own, HEAD)], 3)

    for seg in (0, 2, 1):
        for b in range(NQ):
            rows = slice(b * BLK, (b + 1) * BLK)
            dp = nt(qd[1, rows, :], kv[seg, 1])
            ds = (ebuf[seg, rows, :] * (dp - deltas[b]) * INV_ROOT).astype(BF)
            dsb[seg, rows, :] = ds
            term = nn(ds, kv[seg, 0])
            if seg == 0:
                dqa[rows, :] = term
            else:
                dqa[rows, :] += term
        if seg == 1:
            dd[0, :, W : 3 * HEAD] = dqa[...].astype(BF)
            part = pl.ds(W, HEAD)
            send(dd.at[0, :, part], dd.at[1, :, part], dds, (1,), sib)
        dk = tn(dsb[seg], qd[0])
        dv = tn(pbuf[seg], qd[1])
        if seg == 1:
            ogr[0] = dk
            ogr[1] = dv
        else:
            hgs[seg // 2, 0] = dk.astype(BF)
            hgs[seg // 2, 1] = dv.astype(BF)
            send(hgs.at[seg // 2], hgr.at[seg // 2], hgm, (seg // 2,), prv if seg == 0 else nxt)

    high = ZH * ROWS

    def pair(own_rows, sib_rows, dy, lo, n):
        yy = yd(dy)
        a = nn(own_rows[:, yy, c].reshape(high, T), dd[0, :, lo : lo + n])
        a += nn(sib_rows[:, yy].reshape(high, T), dd[1, :, lo : lo + n])
        return a.reshape(ZH, ROWS, n)

    def term_at(h, dy):
        if h == 0:
            g[0, dy % Y] = pair(ntr, nts, dy, 0, W)
        else:
            g[1, dy % Y, :, :, :HEAD] = pair(ntr, nts, dy, W, HEAD)
            g[1, dy % Y, :, :, HEAD:] = pair(utr, uts, dy, W + HEAD, HEAD)

    def zrange(q):
        return pl.ds(q * ZP, ZP)

    def rs_terms(h, t):
        term_at(h, H - t)
        if t > 0:
            term_at(h, t - H)
        if t == H - 1:
            term_at(h, 0)

    def rs_step(h, t):
        for q in range(2):
            for d in range(2):
                s = 1 if d == 0 else -1
                if t == 0 and q != d:
                    continue
                val = g[h, (s * (H - t)) % Y, zrange(q)]
                if t > 1 or (t == 1 and q == d):
                    arrived(rsr.at[h, d, t - 1, q], rsm, (h, d, t - 1, q))
                    val += rsr[h, d, t - 1, q].astype(F32)
                rss[h, d, t, q] = val.astype(BF)
                send(rss.at[h, d, t, q], rsr.at[h, d, t, q], rsm, (h, d, t, q), ydev(s))

    def rs_last(h):
        for q in range(2):
            val = g[h, 0, zrange(q)]
            for d in range(2):
                arrived(rsr.at[h, d, H - 1, q], rsm, (h, d, H - 1, q))
                val += rsr[h, d, H - 1, q].astype(F32)
            fin[h, zrange(q)] = val
        for k in (2, 1, 3)[: ZH - 1] if ZH == 4 else range(1, ZH):
            zs[h, k] = fin[h, zk(k)].astype(BF)
            send(zs.at[h, k], zr.at[h, k], zsm, (h, k), {"zh": zk(k)})

    def rs_end(h):
        val = fin[h, zh]
        for k in range(1, ZH):
            arrived(zr.at[h, k], zsm, (h, k))
            val += zr[h, k].astype(F32)
        return val

    def wof_part(o, core):
        return wof.at[:, :, core, :, lanes(o, HEAD)]

    def wof_pass():
        for j in range(1, NOWN):
            part = wof_part(owner(NOWN - j), c)
            rcopy(part, part, wos, (j,), sib).wait_recv()
            send(part, part, wps, (j,), sib)

    def mix_wait():
        keep_wo.wait()
        keep_att.wait()
        for j in range(1, NOWN):
            o = owner(NOWN - j)
            arrived(wof_part(o, 1 - c), wps, (j,))
            arrived(att_all.at[:, lanes(o, HEAD)], ats, (j,))

    def mix(z):
        n = D // ZH
        w = wof[z].reshape(n, NOWN * HEAD)
        for b in range(NQ):
            rows = slice(b * BLK, (b + 1) * BLK)
            mixed[rows, z * n : (z + 1) * n] = nt(att_all[rows, :], w).astype(BF)

    arrived(uts, tsw, (0,))
    arrived(nts, tsw, (1,))
    arrived(dd.at[1, :, pl.ds(3 * HEAD, HEAD)], dds, (0,))
    arrived(dd.at[1, :, pl.ds(W, HEAD)], dds, (1,))
    rs_terms(1, 0)
    rs_step(1, 0)
    rs_terms(1, 1)
    for side in range(2):
        arrived(hgr.at[side], hgm, (side,))
    for j in range(2):
        both = ogr[j] + hgr[0, j].astype(F32) + hgr[1, j].astype(F32)
        dd[0, :, j * HEAD : (j + 1) * HEAD] = both.astype(BF)
    send(dd.at[0, :, pl.ds(0, W)], dd.at[1, :, pl.ds(0, W)], dds, (2,), sib)
    rs_step(1, 1)
    rs_terms(1, 2)
    arrived(dd.at[1, :, pl.ds(0, W)], dds, (2,))
    rs_terms(0, 0)
    rs_step(0, 0)
    rs_terms(0, 1)
    for t in range(2, H):
        rs_step(1, t)
        rs_terms(1, t + 1) if t + 1 < H else None
        rs_step(0, t - 1)
        rs_terms(0, t)
        if t == 2:
            wof_pass()
    rs_last(1)
    rs_step(0, H - 1)
    mix_wait()
    for z in range(ZH // 2):
        mix(z)
    rs_last(0)
    for z in range(ZH // 2, ZH):
        mix(z)
    early = rs_end(1)
    gq[0] = early[:, :HEAD]
    go[...] = early[:, HEAD:]
    late = rs_end(0)
    gq[1] = late[:, :HEAD]
    gq[2] = late[:, HEAD:]
    part = wbuf.at[:, :, c, :, pl.ds(3 * HEAD, HEAD)]
    for j in range(1, NOWN):
        rcopy(part, wof_part(own, c), wos, (j,), odev(owner(j))).wait_send()
    finish()


def per_device(
    dims,
    tokens, norm_gain, qkv_codes, qkv_scales, out_codes, out_scales, block_mask, key_counts, upstream,
):
    ZH, Y, ZL, X = dims
    H = Y // 2
    NOWN = ZL * X
    T, D = tokens.shape
    W = 2 * HEAD
    vmem = pl.BlockSpec(memory_space=pltpu.VMEM)
    far = pl.BlockSpec(memory_space=pltpu.HBM)
    buffers = [
        ((T, D), BF),
        ((T, D), BF),
        ((9, T), F32),
        ((T, D), BF),
        ((ZH, Y, 2, ROWS, T), BF),
        ((ZH, Y, 2, ROWS, T), BF),
        ((ZH, Y, ROWS, T), BF),
        ((ZH, Y, ROWS, T), BF),
        ((ZH, Y, 2, ROWS, COLS), BF),
        ((ZH, Y, 2, ROWS, NOWN * HEAD), BF),
        ((2, T, HEAD), BF),
        ((3, 2, T, HEAD), BF),
        ((3, T, T), F32),
        ((3, T, T), BF),
        ((3, T, T), BF),
        ((T, HEAD), F32),
        ((T, HEAD), BF),
        ((T, NOWN * HEAD), BF),
        ((2, 2, T, HEAD), BF),
        ((2, 2, T, HEAD), BF),
        ((2, T, HEAD), F32),
        ((2, T, COLS), BF),
        ((2, Y, ZH, ROWS, W), F32),
        ((2, 2, H, 2, ZH // 2, ROWS, W), BF),
        ((2, 2, H, 2, ZH // 2, ROWS, W), BF),
        ((2, ZH, ROWS, W), F32),
        ((2, ZH, ROWS, W), BF),
        ((2, ZH, ROWS, W), BF),
    ]
    sems = [
        (2, 2, ZH), (2, 2, H, 2, 2), (2, 2, Y), (2, 2, 2), (2, 2), (2, NOWN), (2, NOWN), (2, NOWN),
        (2, 2), (2, 3), (2, 2, 2, H, 2), (2, 2, ZH), (4,),
    ]
    mixed, gq, go = pl.pallas_call(
        functools.partial(kernel, dims),
        out_shape=(
            jax.ShapeDtypeStruct((T, D), BF),
            jax.ShapeDtypeStruct((3, ROWS, HEAD), F32),
            jax.ShapeDtypeStruct((ROWS, HEAD), F32),
        ),
        in_specs=[far] + [vmem] * 7 + [far],
        out_specs=(vmem,) * 3,
        scratch_shapes=[pltpu.VMEM(s, t) for s, t in buffers]
        + [pltpu.SemaphoreType.DMA(s) for s in sems],
        compiler_params=pltpu.CompilerParams(
            collective_id=0, has_side_effects=True, vmem_limit_bytes=63 * 1024 * 1024
        ),
        cost_estimate=pl.CostEstimate(
            flops=4_000_000_000, bytes_accessed=6_000_000, transcendentals=500_000
        ),
    )(
        tokens,
        norm_gain.reshape(1, D),
        qkv_codes.transpose(1, 0, 2),
        qkv_scales.transpose(1, 2, 0),
        out_codes,
        out_scales.transpose(1, 0),
        block_mask,
        key_counts.reshape(1, -1),
        upstream,
    )
    return mixed, gq.transpose(1, 0, 2), go


def build(torus):
    s = torus.shape
    dims = (s["zh"], s["y"], s["zl"], s["x"])
    placed = (
        P(DP, None), P(), P(DP, None, OWN), P(DP, None, OWN), P(DP, OWN), P(DP, OWN), P(DP, None),
        P(), P(DP, None),
    )
    return jax.shard_map(
        functools.partial(per_device, dims),
        mesh=torus,
        in_specs=placed,
        out_specs=(P(DP, None), P(DP, None, OWN), P(DP, OWN)),
        check_vma=False,
    )


def solution(mesh):
    return build(Mesh(mesh.devices.reshape(4, 8, 2, 2, 4), AXES))
```

```python
import functools
import math

import jax
import jax.numpy as jnp
from jax import lax
from jax.experimental import pallas as pl
from jax.experimental.pallas import tpu as pltpu
from jax.sharding import Mesh
from jax.sharding import PartitionSpec as P

HEAD = 128
BLK = 128
ROWS = 32
COLS = 4 * HEAD
AXES = ("zh", "y", "core", "zl", "x")
DP = ("zh", "y", "core")
OWN = ("zl", "x")
BF = jnp.bfloat16
F32 = jnp.float32
MESH = pl.DeviceIdType.MESH
INV_ROOT = 1.0 / HEAD**0.5
TO_EXP2 = INV_ROOT * math.log2(math.e)


def nn(a, b):
    return lax.dot_general(a, b, (((1,), (0,)), ((), ())), preferred_element_type=F32)


def nt(a, b):
    return lax.dot_general(a, b, (((1,), (1,)), ((), ())), preferred_element_type=F32)


def tn(a, b):
    return lax.dot_general(a, b, (((0,), (0,)), ((), ())), preferred_element_type=F32)


def kernel(
    dims,
    tok_hbm, gain, codes, scales, ocodes, oscales, maskb, counts, ups_hbm,
    mixed, gq, go,
    tok, ups, bias, normed, ntr, utr, nts, uts, wbuf, wof, qd, kv, ebuf, pbuf, dsb, dqa, atts,
    att_all, hgs, hgr, ogr, dd, g, rss, rsr, fin, zs, zr,
    agz, agy, ags, halo, tsw, wos, wps, ats, hgm, dds, rsm, zsm, loc,
):
    ZH, Y, ZL, X = dims
    H = Y // 2
    ZP = ZH // 2
    W = 2 * HEAD
    NOWN = ZL * X
    T, D = tok.shape
    NQ = T // BLK
    SEG = T // BLK
    zh, y, c = lax.axis_index("zh"), lax.axis_index("y"), lax.axis_index("core")
    own = lax.axis_index("zl") * X + lax.axis_index("x")
    sib = {"core": 1 - c}
    pending = {}
    locals_ = []

    def rcopy(src, dst, sems, index, dev):
        return pltpu.make_async_remote_copy(
            src_ref=src,
            dst_ref=dst,
            send_sem=sems.at[(0, *index)],
            recv_sem=sems.at[(1, *index)],
            device_id=dev,
            device_id_type=MESH,
        )

    def send(src, dst, sems, index, dev):
        cp = rcopy(src, dst, sems, index, dev)
        cp.start()
        pending[id(sems), index] = [cp, True]

    def arrived(dst, sems, index):
        rcopy(dst, dst, sems, index, sib).wait_recv()
        pending[id(sems), index][1] = False

    def finish():
        for cp in locals_:
            cp.wait()
        for cp, due in pending.values():
            if due:
                cp.wait_recv()
            cp.wait_send()

    def keep(src, dst, i):
        cp = pltpu.make_async_copy(src, dst, loc.at[i])
        cp.start()
        return cp

    def zk(k):
        return lax.rem(zh + k, ZH)

    def yd(d):
        return lax.rem(y + (d + Y), Y)

    def ydev(d):
        return {"y": yd(d)}

    def owner(j):
        return lax.rem(own + j, NOWN)

    def odev(o):
        return {"zl": o // X, "x": lax.rem(o, X)}

    def lanes(o, n):
        return pl.ds(pl.multiple_of(o * n, n), n)

    place = (zh * Y + y) * 2 + c
    count = ZH * Y * 2

    def range_dev(step):
        r = lax.rem(place + step + count, count)
        return {"zh": r // (2 * Y), "y": lax.rem(r // 2, Y), "core": lax.rem(r, 2)}

    nxt, prv = range_dev(1), range_dev(-1)

    barrier = pltpu.get_barrier_semaphore()
    partners = [odev(owner(j)) for j in range(1, NOWN)]
    partners += [{"zh": zk(k)} for k in range(1, ZH)]
    partners += [nxt, prv, ydev(2), ydev(-2), ydev(1), ydev(-1), sib]
    for dev in partners:
        pl.semaphore_signal(barrier, inc=1, device_id=dev, device_id_type=MESH)
    load_tok = keep(tok_hbm, tok, 0)
    load_ups = keep(ups_hbm, ups, 1)

    eye = lax.broadcasted_iota(jnp.int32, (ROWS, ROWS), 0) == lax.broadcasted_iota(
        jnp.int32, (ROWS, ROWS), 1
    )

    def column(row):
        return jnp.sum(jnp.where(eye, row, 0.0), axis=1, keepdims=True)

    for at, j in enumerate((1, 2, 0)):
        part = codes[j].astype(F32) * column(scales[j])
        lo = (at % 2) * HEAD
        wbuf[at // 2, zh, y, c, :, lo : lo + HEAD] = part.astype(BF)
    part = ocodes[...].astype(F32) * column(oscales[...])
    wbuf[1, zh, y, c, :, HEAD:] = part.astype(BF)

    blocks = lax.broadcasted_iota(jnp.int32, counts.shape, 1)
    within = lax.broadcasted_iota(jnp.int32, (1, BLK), 1)
    for j in range(3 * SEG):
        which = place * SEG + (j - SEG)
        alive = jnp.sum(jnp.where(blocks == which, counts[...], 0), axis=1, keepdims=True)
        for b in range(NQ):
            ok = jnp.logical_and(within < alive, maskb[b : b + 1, j : j + 1] > 0)
            row = b * 3 + j // SEG
            lo = (j % SEG) * BLK
            bias[row : row + 1, lo : lo + BLK] = jnp.where(ok, 0.0, -1e30)
    pl.semaphore_wait(barrier, len(partners))

    def piece(h, q, d):
        return wbuf.at[h, pl.ds(q * ZP, ZP), yd(d), c]

    def ag_send(d, t, h, q):
        s = 1 if d == 0 else -1
        b = piece(h, q, -s * (t - 1))
        send(b, b, agy, (d, t - 1, h, q), ydev(s))

    def ag_skip(d, h, q):
        s = 1 if d == 0 else -1
        b = piece(h, q, -s * (H - 2))
        send(b, b, agy, (d, H - 1, h, q), ydev(2 * s))

    def ag_wait(d, t, h, q):
        s = 1 if d == 0 else -1
        arrived(piece(h, q, -s * t), agy, (d, t - 1, h, q))

    def ag_pass(h, dy):
        b = wbuf.at[h, :, yd(dy), c]
        send(b, b, ags, (h, dy % Y), sib)

    def wof_send(dy):
        src = wbuf.at[1, :, yd(dy), c, :, pl.ds(HEAD, HEAD)]
        for j in range(1, NOWN):
            o = owner(j)
            rcopy(src, wof.at[:, yd(dy), c, :, lanes(own, HEAD)], wos, (j,), odev(o)).start()

    def ag_z(h):
        for k in range(1, ZH):
            arrived(wbuf.at[h, zk(ZH - k), y, c], agz, (h, k))
        for q in range(2):
            for d in range(2):
                ag_send(d, 1, h, q)
        ag_pass(h, 0)

    for h in range(2):
        mine = wbuf.at[h, zh, y, c]
        for k in (2, 1, 3)[: ZH - 1] if ZH == 4 else range(1, ZH):
            send(mine, mine, agz, (h, k), {"zh": zk(k)})

    def norm_rows(i, carry):
        r = pl.ds(pl.multiple_of(i * 16, 16), 16)
        x = tok[r, :].astype(F32)
        factor = lax.rsqrt(jnp.mean(x * x, axis=-1, keepdims=True) + 1e-05)
        normed[r, :] = (x * factor * gain[...]).astype(BF)
        return carry

    def turn(src, dst):
        per = Y // 2

        def body(j, carry):
            v = src[:, pl.ds(pl.multiple_of(j * 128, 128), 128)]
            dst[j // per, pl.ds(2 * lax.rem(j, per), 2)] = v.T.reshape(2, 2, ROWS, T)
            return carry

        return body

    load_tok.wait()
    lax.fori_loop(0, T // 16, norm_rows, 0)
    ag_z(0)
    ag_z(1)
    wof_send(0)
    load_ups.wait()

    def fill(t):
        if t == 1:
            lax.fori_loop(0, D // 128, turn(ups, utr), 0)
            send(utr.at[:, :, 1 - c], uts, tsw, (0,), sib)
        if t == 2:
            lax.fori_loop(0, D // 128, turn(normed, ntr), 0)
            send(ntr.at[:, :, 1 - c], nts, tsw, (1,), sib)

    for t in range(1, H):
        for h in range(2):
            for q in range(2):
                for d in range(2):
                    ag_wait(d, t, h, q)
                    if t < H - 1:
                        ag_send(d, t + 1, h, q)
                    if t == H - 2 and q == d:
                        ag_skip(d, h, q)
            ag_pass(h, -t)
            ag_pass(h, t)
            if t == H - 1:
                for d in range(2):
                    ag_wait(d, H, h, d)
                ag_pass(h, H)
        wof_send(-t)
        wof_send(t)
        if t == H - 1:
            wof_send(H)
        fill(t)

    def from_sibling(h):
        for dy in range(Y):
            arrived(wbuf.at[h, :, yd(dy), 1 - c], ags, (h, dy))

    def project(src, h, lo, n):
        total = None
        for z in range(ZH):
            w = wbuf[h, z, :, :, :, lo : lo + n].reshape(Y * 2 * ROWS, n)
            term = nn(src[:, z * Y * 64 : (z + 1) * Y * 64], w)
            total = term if total is None else total + term
        return total.astype(BF)

    from_sibling(0)
    keyval = project(normed, 0, 0, W)
    kv[1, 0] = keyval[:, :HEAD]
    kv[1, 1] = keyval[:, HEAD:]
    for j in range(2):
        send(kv.at[1, j], kv.at[0, j], halo, (0, j), nxt)
        send(kv.at[1, j], kv.at[2, j], halo, (1, j), prv)
    from_sibling(1)
    qd[0] = project(normed, 1, 0, HEAD)
    qd[1] = project(ups, 1, HEAD, HEAD)
    keep_wo = keep(
        wbuf.at[1, :, :, :, :, pl.ds(HEAD, HEAD)], wof.at[:, :, :, :, lanes(own, HEAD)], 2
    )

    sums = [None] * NQ
    for seg in (1, 0, 2):
        if seg != 1:
            arrived(kv.at[seg, 0], halo, (seg // 2, 0))
        for b in range(NQ):
            rows = slice(b * BLK, (b + 1) * BLK)
            score = nt(qd[0, rows, :], kv[seg, 0])
            e = jnp.exp2(score * TO_EXP2 + bias[b * 3 + seg : b * 3 + seg + 1, :])
            ebuf[seg, rows, :] = e
            part = jnp.sum(e, axis=-1, keepdims=True)
            sums[b] = part if sums[b] is None else sums[b] + part
    for seg in (0, 2):
        arrived(kv.at[seg, 1], halo, (seg // 2, 1))
    deltas = []
    for b in range(NQ):
        rows = slice(b * BLK, (b + 1) * BLK)
        scale = 1.0 / sums[b]
        total = None
        for seg in range(3):
            p = ebuf[seg, rows, :] * scale
            ebuf[seg, rows, :] = p
            pb = p.astype(BF)
            pbuf[seg, rows, :] = pb
            term = nn(pb, kv[seg, 1])
            total = term if total is None else total + term
        atts[rows, :] = total.astype(BF)
        deltas.append(jnp.sum(total * qd[1, rows, :].astype(F32), axis=-1, keepdims=True))
    dd[0, :, 3 * HEAD :] = atts[...]
    send(dd.at[0, :, pl.ds(3 * HEAD, HEAD)], dd.at[1, :, pl.ds(3 * HEAD, HEAD)], dds, (0,), sib)
    for j in range(1, NOWN):
        send(atts, att_all.at[:, lanes(own, HEAD)], ats, (j,), odev(owner(j)))
    keep_att = keep(atts, att_all.at[:, lanes(own, HEAD)], 3)

    for seg in (0, 2, 1):
        for b in range(NQ):
            rows = slice(b * BLK, (b + 1) * BLK)
            dp = nt(qd[1, rows, :], kv[seg, 1])
            ds = (ebuf[seg, rows, :] * (dp - deltas[b]) * INV_ROOT).astype(BF)
            dsb[seg, rows, :] = ds
            term = nn(ds, kv[seg, 0])
            if seg == 0:
                dqa[rows, :] = term
            else:
                dqa[rows, :] += term
        if seg == 1:
            dd[0, :, W : 3 * HEAD] = dqa[...].astype(BF)
            part = pl.ds(W, HEAD)
            send(dd.at[0, :, part], dd.at[1, :, part], dds, (1,), sib)
        dk = tn(dsb[seg], qd[0])
        dv = tn(pbuf[seg], qd[1])
        if seg == 1:
            ogr[0] = dk
            ogr[1] = dv
        else:
            hgs[seg // 2, 0] = dk.astype(BF)
            hgs[seg // 2, 1] = dv.astype(BF)
            send(hgs.at[seg // 2], hgr.at[seg // 2], hgm, (seg // 2,), prv if seg == 0 else nxt)

    high = ZH * ROWS

    def pair(own_rows, sib_rows, dy, lo, n):
        yy = yd(dy)
        a = nn(own_rows[:, yy, c].reshape(high, T), dd[0, :, lo : lo + n])
        a += nn(sib_rows[:, yy].reshape(high, T), dd[1, :, lo : lo + n])
        return a.reshape(ZH, ROWS, n)

    def term_at(h, dy):
        if h == 0:
            g[0, dy % Y] = pair(ntr, nts, dy, 0, W)
        else:
            g[1, dy % Y, :, :, :HEAD] = pair(ntr, nts, dy, W, HEAD)
            g[1, dy % Y, :, :, HEAD:] = pair(utr, uts, dy, W + HEAD, HEAD)

    def zrange(q):
        return pl.ds(q * ZP, ZP)

    def rs_terms(h, t):
        for dy in {0: (H, H - 1, 1 - H), 1: (H - 2, 2 - H), 2: (1, -1, 0)}[t]:
            term_at(h, dy)

    def rs_send(val, h, d, t, q, hops):
        rss[h, d, t, q] = val.astype(BF)
        send(rss.at[h, d, t, q], rsr.at[h, d, t, q], rsm, (h, d, t, q), ydev(hops))

    def rs_got(h, d, t, q):
        arrived(rsr.at[h, d, t, q], rsm, (h, d, t, q))
        return rsr[h, d, t, q].astype(F32)

    def rs_step(h, t):
        for q in range(2):
            for d in range(2):
                s = 1 if d == 0 else -1
                far = H - 1 - t
                val = g[h, (s * far) % Y, zrange(q)]
                if t == 0:
                    if q == d:
                        rs_send(g[h, H, zrange(q)], h, d, 0, q, 2 * s)
                else:
                    val += rs_got(h, d, t, q)
                    if t == 1 and q == d:
                        val += rs_got(h, d, 0, q)
                rs_send(val, h, d, t + 1, q, s)

    def rs_last(h):
        for q in range(2):
            val = g[h, 0, zrange(q)]
            for d in range(2):
                arrived(rsr.at[h, d, H - 1, q], rsm, (h, d, H - 1, q))
                val += rsr[h, d, H - 1, q].astype(F32)
            fin[h, zrange(q)] = val
        for k in (2, 1, 3)[: ZH - 1] if ZH == 4 else range(1, ZH):
            zs[h, k] = fin[h, zk(k)].astype(BF)
            send(zs.at[h, k], zr.at[h, k], zsm, (h, k), {"zh": zk(k)})

    def rs_end(h):
        val = fin[h, zh]
        for k in range(1, ZH):
            arrived(zr.at[h, k], zsm, (h, k))
            val += zr[h, k].astype(F32)
        return val

    def wof_part(o, core):
        return wof.at[:, :, core, :, lanes(o, HEAD)]

    def wof_pass():
        for j in range(1, NOWN):
            part = wof_part(owner(NOWN - j), c)
            rcopy(part, part, wos, (j,), sib).wait_recv()
            send(part, part, wps, (j,), sib)

    def mix_wait():
        keep_wo.wait()
        keep_att.wait()
        for j in range(1, NOWN):
            o = owner(NOWN - j)
            arrived(wof_part(o, 1 - c), wps, (j,))
            arrived(att_all.at[:, lanes(o, HEAD)], ats, (j,))

    def mix(z):
        n = D // ZH
        w = wof[z].reshape(n, NOWN * HEAD)
        for b in range(NQ):
            rows = slice(b * BLK, (b + 1) * BLK)
            mixed[rows, z * n : (z + 1) * n] = nt(att_all[rows, :], w).astype(BF)

    arrived(uts, tsw, (0,))
    arrived(nts, tsw, (1,))
    arrived(dd.at[1, :, pl.ds(3 * HEAD, HEAD)], dds, (0,))
    arrived(dd.at[1, :, pl.ds(W, HEAD)], dds, (1,))
    rs_terms(1, 0)
    rs_step(1, 0)
    rs_terms(1, 1)
    for side in range(2):
        arrived(hgr.at[side], hgm, (side,))
    for j in range(2):
        both = ogr[j] + hgr[0, j].astype(F32) + hgr[1, j].astype(F32)
        dd[0, :, j * HEAD : (j + 1) * HEAD] = both.astype(BF)
    send(dd.at[0, :, pl.ds(0, W)], dd.at[1, :, pl.ds(0, W)], dds, (2,), sib)
    rs_step(1, 1)
    rs_terms(1, 2)
    arrived(dd.at[1, :, pl.ds(0, W)], dds, (2,))
    rs_terms(0, 0)
    rs_step(0, 0)
    rs_terms(0, 1)
    rs_step(1, 2)
    rs_terms(0, 2)
    rs_step(0, 1)
    wof_pass()
    rs_last(1)
    rs_step(0, 2)
    mix_wait()
    for z in range(ZH // 2):
        mix(z)
    rs_last(0)
    for z in range(ZH // 2, ZH):
        mix(z)
    early = rs_end(1)
    gq[0] = early[:, :HEAD]
    go[...] = early[:, HEAD:]
    late = rs_end(0)
    gq[1] = late[:, :HEAD]
    gq[2] = late[:, HEAD:]
    part = wbuf.at[1, :, :, c, :, pl.ds(HEAD, HEAD)]
    for j in range(1, NOWN):
        rcopy(part, wof_part(own, c), wos, (j,), odev(owner(j))).wait_send()
    finish()


def store(*refs):
    sources, results, held, sems = refs[:3], refs[3:6], refs[6:9], refs[9]
    rows = sources[0].shape[0] // 4
    parts = [(0, pl.ds(i * rows, rows)) for i in range(4)] + [(1, slice(None)), (2, slice(None))]
    inward, outward = [], []
    for i, (a, part) in enumerate(parts):
        inward.append(
            pltpu.make_async_copy(sources[a].at[part], held[a].at[part], sems.at[0, i])
        )
        outward.append(
            pltpu.make_async_copy(held[a].at[part], results[a].at[part], sems.at[1, i])
        )
        inward[-1].start()
    for first, second in zip(inward, outward):
        first.wait()
        second.start()
    for second in outward:
        second.wait()


def per_device(
    dims,
    tokens, norm_gain, qkv_codes, qkv_scales, out_codes, out_scales, block_mask, key_counts, upstream,
):
    ZH, Y, ZL, X = dims
    H = Y // 2
    NOWN = ZL * X
    T, D = tokens.shape
    W = 2 * HEAD
    vmem = pl.BlockSpec(memory_space=pltpu.VMEM)
    far = pl.BlockSpec(memory_space=pltpu.HBM)
    buffers = [
        ((T, D), BF),
        ((T, D), BF),
        ((9, T), F32),
        ((T, D), BF),
        ((ZH, Y, 2, ROWS, T), BF),
        ((ZH, Y, 2, ROWS, T), BF),
        ((ZH, Y, ROWS, T), BF),
        ((ZH, Y, ROWS, T), BF),
        ((2, ZH, Y, 2, ROWS, W), BF),
        ((ZH, Y, 2, ROWS, NOWN * HEAD), BF),
        ((2, T, HEAD), BF),
        ((3, 2, T, HEAD), BF),
        ((3, T, T), F32),
        ((3, T, T), BF),
        ((3, T, T), BF),
        ((T, HEAD), F32),
        ((T, HEAD), BF),
        ((T, NOWN * HEAD), BF),
        ((2, 2, T, HEAD), BF),
        ((2, 2, T, HEAD), BF),
        ((2, T, HEAD), F32),
        ((2, T, COLS), BF),
        ((2, Y, ZH, ROWS, W), F32),
        ((2, 2, H, 2, ZH // 2, ROWS, W), BF),
        ((2, 2, H, 2, ZH // 2, ROWS, W), BF),
        ((2, ZH, ROWS, W), F32),
        ((2, ZH, ROWS, W), BF),
        ((2, ZH, ROWS, W), BF),
    ]
    sems = [
        (2, 2, ZH), (2, 2, H, 2, 2), (2, 2, Y), (2, 2, 2), (2, 2), (2, NOWN), (2, NOWN), (2, NOWN),
        (2, 2), (2, 3), (2, 2, 2, H, 2), (2, 2, ZH), (4,),
    ]
    mixed, gq, go = pl.pallas_call(
        functools.partial(kernel, dims),
        out_shape=(
            jax.ShapeDtypeStruct((T, D), BF),
            jax.ShapeDtypeStruct((3, ROWS, HEAD), F32),
            jax.ShapeDtypeStruct((ROWS, HEAD), F32),
        ),
        in_specs=[far] + [vmem] * 7 + [far],
        out_specs=(vmem,) * 3,
        scratch_shapes=[pltpu.VMEM(s, t) for s, t in buffers]
        + [pltpu.SemaphoreType.DMA(s) for s in sems],
        compiler_params=pltpu.CompilerParams(
            collective_id=0, has_side_effects=True, vmem_limit_bytes=63 * 1024 * 1024
        ),
        cost_estimate=pl.CostEstimate(
            flops=4_000_000_000, bytes_accessed=6_000_000, transcendentals=500_000
        ),
    )(
        tokens,
        norm_gain.reshape(1, D),
        qkv_codes.transpose(1, 0, 2),
        qkv_scales.transpose(1, 2, 0),
        out_codes,
        out_scales.transpose(1, 0),
        block_mask,
        key_counts.reshape(1, -1),
        upstream,
    )
    mixed, gq, go = pl.pallas_call(
        store,
        out_shape=tuple(jax.ShapeDtypeStruct(a.shape, a.dtype) for a in (mixed, gq, go)),
        in_specs=[far] * 3,
        out_specs=(far,) * 3,
        scratch_shapes=[pltpu.VMEM(a.shape, a.dtype) for a in (mixed, gq, go)]
        + [pltpu.SemaphoreType.DMA((2, 6))],
        compiler_params=pltpu.CompilerParams(vmem_limit_bytes=63 * 1024 * 1024),
    )(mixed, gq, go)
    return mixed, gq.transpose(1, 0, 2), go


def build(torus):
    s = torus.shape
    dims = (s["zh"], s["y"], s["zl"], s["x"])
    placed = (
        P(DP, None), P(), P(DP, None, OWN), P(DP, None, OWN), P(DP, OWN), P(DP, OWN), P(DP, None),
        P(), P(DP, None),
    )
    return jax.shard_map(
        functools.partial(per_device, dims),
        mesh=torus,
        in_specs=placed,
        out_specs=(P(DP, None), P(DP, None, OWN), P(DP, OWN)),
        check_vma=False,
    )


def solution(mesh):
    return build(Mesh(mesh.devices.reshape(4, 8, 2, 2, 4), AXES))
```

```python
import functools
import math

import jax
import jax.numpy as jnp
from jax import lax
from jax.experimental import pallas as pl
from jax.experimental.pallas import tpu as pltpu
from jax.sharding import Mesh
from jax.sharding import PartitionSpec as P

HEAD = 128
BLK = 128
ROWS = 32
COLS = 4 * HEAD
AXES = ("zh", "y", "core", "zl", "x")
DP = ("zh", "y", "core")
OWN = ("zl", "x")
BF = jnp.bfloat16
F32 = jnp.float32
MESH = pl.DeviceIdType.MESH
INV_ROOT = 1.0 / HEAD**0.5
TO_EXP2 = INV_ROOT * math.log2(math.e)


def nn(a, b):
    return lax.dot_general(a, b, (((1,), (0,)), ((), ())), preferred_element_type=F32)


def nt(a, b):
    return lax.dot_general(a, b, (((1,), (1,)), ((), ())), preferred_element_type=F32)


def tn(a, b):
    return lax.dot_general(a, b, (((0,), (0,)), ((), ())), preferred_element_type=F32)


def kernel(
    dims,
    tok_hbm, gain, codes, scales, ocodes, oscales, maskb, counts, ups_hbm,
    mixed, gq, go,
    tok, ups, bias, normed, ntr, utr, nts, uts, wbuf, wof, qd, kv, ebuf, pbuf, dsb, atts,
    att_all, mixv, hgs, hgr, ogr, dd, g, rss, rsr, fin, zs, zr,
    agz, agy, ags, halo, tsw, wos, wps, ats, hgm, dds, rsm, zsm, loc,
):
    ZH, Y, ZL, X = dims
    H = Y // 2
    ZP = ZH // 2
    W = 2 * HEAD
    NOWN = ZL * X
    T, D = tok.shape
    NQ = T // BLK
    SEG = T // BLK
    zh, y, c = lax.axis_index("zh"), lax.axis_index("y"), lax.axis_index("core")
    own = lax.axis_index("zl") * X + lax.axis_index("x")
    sib = {"core": 1 - c}
    pending = {}
    locals_ = []

    def rcopy(src, dst, sems, index, dev):
        return pltpu.make_async_remote_copy(
            src_ref=src,
            dst_ref=dst,
            send_sem=sems.at[(0, *index)],
            recv_sem=sems.at[(1, *index)],
            device_id=dev,
            device_id_type=MESH,
        )

    def send(src, dst, sems, index, dev):
        cp = rcopy(src, dst, sems, index, dev)
        cp.start()
        pending[id(sems), index] = [cp, True]

    def arrived(dst, sems, index):
        rcopy(dst, dst, sems, index, sib).wait_recv()
        pending[id(sems), index][1] = False

    def finish():
        for cp in locals_:
            cp.wait()
        for cp, due in pending.values():
            if due:
                cp.wait_recv()
            cp.wait_send()

    def keep(src, dst, i):
        cp = pltpu.make_async_copy(src, dst, loc.at[i])
        cp.start()
        return cp

    def zk(k):
        return lax.rem(zh + k, ZH)

    def yd(d):
        return lax.rem(y + (d + Y), Y)

    def ydev(d):
        return {"y": yd(d)}

    def owner(j):
        return lax.rem(own + j, NOWN)

    def odev(o):
        return {"zl": o // X, "x": lax.rem(o, X)}

    def lanes(o, n):
        return pl.ds(pl.multiple_of(o * n, n), n)

    place = (zh * Y + y) * 2 + c
    count = ZH * Y * 2

    def range_dev(step):
        r = lax.rem(place + step + count, count)
        return {"zh": r // (2 * Y), "y": lax.rem(r // 2, Y), "core": lax.rem(r, 2)}

    nxt, prv = range_dev(1), range_dev(-1)

    barrier = pltpu.get_barrier_semaphore()
    partners = [odev(owner(j)) for j in range(1, NOWN)]
    partners += [{"zh": zk(k)} for k in range(1, ZH)]
    partners += [nxt, prv, ydev(2), ydev(-2), ydev(1), ydev(-1)]
    for dev in partners:
        pl.semaphore_signal(barrier, inc=1, device_id=dev, device_id_type=MESH)
    load_tok = keep(tok_hbm, tok, 0)
    load_ups = keep(ups_hbm, ups, 1)

    eye = lax.broadcasted_iota(jnp.int32, (ROWS, ROWS), 0) == lax.broadcasted_iota(
        jnp.int32, (ROWS, ROWS), 1
    )

    def column(row):
        return jnp.sum(jnp.where(eye, row, 0.0), axis=1, keepdims=True)

    for at, j in enumerate((1, 2, 0)):
        part = codes[j].astype(F32) * column(scales[j])
        lo = (at % 2) * HEAD
        wbuf[at // 2, zh, y, c, :, lo : lo + HEAD] = part.astype(BF)
    part = ocodes[...].astype(F32) * column(oscales[...])
    wbuf[1, zh, y, c, :, HEAD:] = part.astype(BF)

    blocks = lax.broadcasted_iota(jnp.int32, counts.shape, 1)
    within = lax.broadcasted_iota(jnp.int32, (1, BLK), 1)
    for j in range(3 * SEG):
        which = place * SEG + (j - SEG)
        alive = jnp.sum(jnp.where(blocks == which, counts[...], 0), axis=1, keepdims=True)
        for b in range(NQ):
            ok = jnp.logical_and(within < alive, maskb[b : b + 1, j : j + 1] > 0)
            row = b * 3 + j // SEG
            lo = (j % SEG) * BLK
            bias[row : row + 1, lo : lo + BLK] = jnp.where(ok, 0.0, -1e30)
    pl.semaphore_wait(barrier, len(partners))

    def piece(h, q, d):
        return wbuf.at[h, pl.ds(q * ZP, ZP), yd(d), c]

    def ag_send(d, t, h, q):
        s = 1 if d == 0 else -1
        b = piece(h, q, -s * (t - 1))
        send(b, b, agy, (d, t - 1, h, q), ydev(s))

    def ag_skip(d, h, q):
        s = 1 if d == 0 else -1
        b = piece(h, q, -s * (H - 2))
        send(b, b, agy, (d, H - 1, h, q), ydev(2 * s))

    def ag_wait(d, t, h, q):
        s = 1 if d == 0 else -1
        arrived(piece(h, q, -s * t), agy, (d, t - 1, h, q))

    def ag_pass(h, dy):
        b = wbuf.at[h, :, yd(dy), c]
        send(b, b, ags, (h, dy % Y), sib)

    def wof_send(dy):
        src = wbuf.at[1, :, yd(dy), c, :, pl.ds(HEAD, HEAD)]
        for j in range(1, NOWN):
            o = owner(j)
            rcopy(src, wof.at[:, yd(dy), c, :, lanes(own, HEAD)], wos, (j,), odev(o)).start()

    def ag_z(h):
        for k in range(1, ZH):
            arrived(wbuf.at[h, zk(ZH - k), y, c], agz, (h, k))
        for q in range(2):
            for d in range(2):
                ag_send(d, 1, h, q)
        ag_pass(h, 0)

    for h in range(2):
        mine = wbuf.at[h, zh, y, c]
        for k in (2, 1, 3)[: ZH - 1] if ZH == 4 else range(1, ZH):
            send(mine, mine, agz, (h, k), {"zh": zk(k)})

    def norm_rows(i, carry):
        r = pl.ds(pl.multiple_of(i * 16, 16), 16)
        x = tok[r, :].astype(F32)
        factor = lax.rsqrt(jnp.mean(x * x, axis=-1, keepdims=True) + 1e-05)
        normed[r, :] = (x * factor * gain[...]).astype(BF)
        return carry

    def turn(src, dst):
        per = Y // 2

        def body(j, carry):
            v = src[:, pl.ds(pl.multiple_of(j * 128, 128), 128)]
            dst[j // per, pl.ds(2 * lax.rem(j, per), 2)] = v.T.reshape(2, 2, ROWS, T)
            return carry

        return body

    load_tok.wait()
    lax.fori_loop(0, T // 16, norm_rows, 0)
    ag_z(0)
    ag_z(1)
    wof_send(0)
    load_ups.wait()

    def fill(t):
        if t == 1:
            lax.fori_loop(0, D // 128, turn(ups, utr), 0)
            send(utr.at[:, :, 1 - c], uts, tsw, (0,), sib)
        if t == 2:
            lax.fori_loop(0, D // 128, turn(normed, ntr), 0)
            send(ntr.at[:, :, 1 - c], nts, tsw, (1,), sib)

    for t in range(1, H):
        for h in range(2):
            for q in range(2):
                for d in range(2):
                    ag_wait(d, t, h, q)
                    if t < H - 1:
                        ag_send(d, t + 1, h, q)
                    if t == H - 2 and q == d:
                        ag_skip(d, h, q)
            ag_pass(h, -t)
            ag_pass(h, t)
            if t == H - 1:
                for d in range(2):
                    ag_wait(d, H, h, d)
                ag_pass(h, H)
        wof_send(-t)
        wof_send(t)
        if t == H - 1:
            wof_send(H)
        fill(t)

    def from_sibling(h):
        for dy in range(Y):
            arrived(wbuf.at[h, :, yd(dy), 1 - c], ags, (h, dy))

    def project(src, h, lo, n):
        total = None
        for z in range(ZH):
            w = wbuf[h, z, :, :, :, lo : lo + n].reshape(Y * 2 * ROWS, n)
            term = nn(src[:, z * Y * 64 : (z + 1) * Y * 64], w)
            total = term if total is None else total + term
        return total.astype(BF)

    from_sibling(0)
    keyval = project(normed, 0, 0, W)
    kv[1, 0] = keyval[:, :HEAD]
    kv[1, 1] = keyval[:, HEAD:]
    for j in range(2):
        send(kv.at[1, j], kv.at[0, j], halo, (0, j), nxt)
        send(kv.at[1, j], kv.at[2, j], halo, (1, j), prv)
    from_sibling(1)
    qd[0] = project(normed, 1, 0, HEAD)
    qd[1] = project(ups, 1, HEAD, HEAD)
    keep_wo = keep(
        wbuf.at[1, :, :, :, :, pl.ds(HEAD, HEAD)], wof.at[:, :, :, :, lanes(own, HEAD)], 2
    )

    sums = [None] * NQ
    for seg in (1, 0, 2):
        if seg != 1:
            arrived(kv.at[seg, 0], halo, (seg // 2, 0))
        for b in range(NQ):
            rows = slice(b * BLK, (b + 1) * BLK)
            score = nt(qd[0, rows, :], kv[seg, 0])
            e = jnp.exp2(score * TO_EXP2 + bias[b * 3 + seg : b * 3 + seg + 1, :])
            ebuf[seg, rows, :] = e
            part = jnp.sum(e, axis=-1, keepdims=True)
            sums[b] = part if sums[b] is None else sums[b] + part
    for seg in (0, 2):
        arrived(kv.at[seg, 1], halo, (seg // 2, 1))
    deltas = []
    for b in range(NQ):
        rows = slice(b * BLK, (b + 1) * BLK)
        scale = 1.0 / sums[b]
        total = None
        for seg in range(3):
            p = ebuf[seg, rows, :] * scale
            ebuf[seg, rows, :] = p
            pb = p.astype(BF)
            pbuf[seg, rows, :] = pb
            term = nn(pb, kv[seg, 1])
            total = term if total is None else total + term
        atts[rows, :] = total.astype(BF)
        deltas.append(jnp.sum(total * qd[1, rows, :].astype(F32), axis=-1, keepdims=True))
    dd[0, :, 3 * HEAD :] = atts[...]
    send(dd.at[0, :, pl.ds(3 * HEAD, HEAD)], dd.at[1, :, pl.ds(3 * HEAD, HEAD)], dds, (0,), sib)
    for j in range(1, NOWN):
        send(atts, att_all.at[:, lanes(own, HEAD)], ats, (j,), odev(owner(j)))
    keep_att = keep(atts, att_all.at[:, lanes(own, HEAD)], 3)

    def to_neighbour(seg, j, value):
        side = seg // 2
        hgs[side, j] = value.astype(BF)
        send(hgs.at[side, j], hgr.at[side, j], hgm, (side, j), prv if seg == 0 else nxt)

    for seg in (0, 2):
        to_neighbour(seg, 1, tn(pbuf[seg], qd[1]))
    for seg in (0, 2, 1):
        for b in range(NQ):
            rows = slice(b * BLK, (b + 1) * BLK)
            dp = nt(qd[1, rows, :], kv[seg, 1])
            dsb[seg, rows, :] = (ebuf[seg, rows, :] * (dp - deltas[b]) * INV_ROOT).astype(BF)
        if seg != 1:
            to_neighbour(seg, 0, tn(dsb[seg], qd[0]))
    for b in range(NQ):
        rows = slice(b * BLK, (b + 1) * BLK)
        total = nn(dsb[0, rows, :], kv[0, 0])
        for seg in (1, 2):
            total += nn(dsb[seg, rows, :], kv[seg, 0])
        dd[0, rows, W : 3 * HEAD] = total.astype(BF)
    part = pl.ds(W, HEAD)
    send(dd.at[0, :, part], dd.at[1, :, part], dds, (1,), sib)
    ogr[0] = tn(dsb[1], qd[0])
    ogr[1] = tn(pbuf[1], qd[1])

    high = ZH * ROWS

    def pair(own_rows, sib_rows, dy, lo, n):
        yy = yd(dy)
        a = nn(own_rows[:, yy, c].reshape(high, T), dd[0, :, lo : lo + n])
        a += nn(sib_rows[:, yy].reshape(high, T), dd[1, :, lo : lo + n])
        return a.reshape(ZH, ROWS, n)

    def term_at(h, dy):
        if h == 0:
            g[0, dy % Y] = pair(ntr, nts, dy, 0, W)
        else:
            g[1, dy % Y, :, :, :HEAD] = pair(ntr, nts, dy, W, HEAD)
            g[1, dy % Y, :, :, HEAD:] = pair(utr, uts, dy, W + HEAD, HEAD)

    def zrange(q):
        return pl.ds(q * ZP, ZP)

    def rs_terms(h, t):
        for dy in {0: (H, H - 1, 1 - H), 1: (H - 2, 2 - H), 2: (1, -1, 0)}[t]:
            term_at(h, dy)

    def rs_send(val, h, d, t, q, hops):
        rss[h, d, t, q] = val.astype(BF)
        send(rss.at[h, d, t, q], rsr.at[h, d, t, q], rsm, (h, d, t, q), ydev(hops))

    def rs_got(h, d, t, q):
        arrived(rsr.at[h, d, t, q], rsm, (h, d, t, q))
        return rsr[h, d, t, q].astype(F32)

    def rs_step(h, t):
        for q in range(2):
            for d in range(2):
                s = 1 if d == 0 else -1
                far = H - 1 - t
                val = g[h, (s * far) % Y, zrange(q)]
                if t == 0:
                    if q == d:
                        rs_send(g[h, H, zrange(q)], h, d, 0, q, 2 * s)
                else:
                    val += rs_got(h, d, t, q)
                    if t == 1 and q == d:
                        val += rs_got(h, d, 0, q)
                rs_send(val, h, d, t + 1, q, s)

    def rs_last(h):
        for q in range(2):
            val = g[h, 0, zrange(q)]
            for d in range(2):
                arrived(rsr.at[h, d, H - 1, q], rsm, (h, d, H - 1, q))
                val += rsr[h, d, H - 1, q].astype(F32)
            fin[h, zrange(q)] = val
        for k in (2, 1, 3)[: ZH - 1] if ZH == 4 else range(1, ZH):
            zs[h, k] = fin[h, zk(k)].astype(BF)
            send(zs.at[h, k], zr.at[h, k], zsm, (h, k), {"zh": zk(k)})

    def rs_end(h):
        val = fin[h, zh]
        for k in range(1, ZH):
            arrived(zr.at[h, k], zsm, (h, k))
            val += zr[h, k].astype(F32)
        return val

    def wof_part(o, core):
        return wof.at[:, :, core, :, lanes(o, HEAD)]

    def wof_pass():
        for j in range(1, NOWN):
            part = wof_part(owner(NOWN - j), c)
            rcopy(part, part, wos, (j,), sib).wait_recv()
            send(part, part, wps, (j,), sib)

    def mix_wait():
        keep_wo.wait()
        keep_att.wait()
        for j in range(1, NOWN):
            o = owner(NOWN - j)
            arrived(wof_part(o, 1 - c), wps, (j,))
            arrived(att_all.at[:, lanes(o, HEAD)], ats, (j,))

    def mix(z):
        n = D // ZH
        w = wof[z].reshape(n, NOWN * HEAD)
        for b in range(NQ):
            rows = slice(b * BLK, (b + 1) * BLK)
            mixv[rows, z * n : (z + 1) * n] = nt(att_all[rows, :], w).astype(BF)
        part = pl.ds(z * n, n)
        locals_.append(keep(mixv.at[:, part], mixed.at[:, part], 4 + z))

    arrived(uts, tsw, (0,))
    arrived(nts, tsw, (1,))
    arrived(dd.at[1, :, pl.ds(3 * HEAD, HEAD)], dds, (0,))
    arrived(dd.at[1, :, pl.ds(W, HEAD)], dds, (1,))
    rs_terms(1, 0)
    rs_step(1, 0)
    rs_terms(1, 1)
    for side in range(2):
        for j in range(2):
            arrived(hgr.at[side, j], hgm, (side, j))
    for j in range(2):
        both = ogr[j] + hgr[0, j].astype(F32) + hgr[1, j].astype(F32)
        dd[0, :, j * HEAD : (j + 1) * HEAD] = both.astype(BF)
    send(dd.at[0, :, pl.ds(0, W)], dd.at[1, :, pl.ds(0, W)], dds, (2,), sib)
    rs_step(1, 1)
    rs_terms(1, 2)
    arrived(dd.at[1, :, pl.ds(0, W)], dds, (2,))
    rs_terms(0, 0)
    rs_step(0, 0)
    rs_terms(0, 1)
    rs_step(1, 2)
    rs_terms(0, 2)
    rs_step(0, 1)
    wof_pass()
    rs_last(1)
    rs_step(0, 2)
    mix_wait()
    for z in range(ZH // 2):
        mix(z)
    rs_last(0)
    for z in range(ZH // 2, ZH):
        mix(z)
    early = rs_end(1)
    gq[0] = early[:, :HEAD]
    go[...] = early[:, HEAD:]
    late = rs_end(0)
    gq[1] = late[:, :HEAD]
    gq[2] = late[:, HEAD:]
    part = wbuf.at[1, :, :, c, :, pl.ds(HEAD, HEAD)]
    for j in range(1, NOWN):
        rcopy(part, wof_part(own, c), wos, (j,), odev(owner(j))).wait_send()
    finish()


def store(*refs):
    sources, results, held, sems = refs[:3], refs[3:6], refs[6:9], refs[9]
    rows = sources[0].shape[0] // 4
    parts = [(0, pl.ds(i * rows, rows)) for i in range(4)] + [(1, slice(None)), (2, slice(None))]
    inward, outward = [], []
    for i, (a, part) in enumerate(parts):
        inward.append(
            pltpu.make_async_copy(sources[a].at[part], held[a].at[part], sems.at[0, i])
        )
        outward.append(
            pltpu.make_async_copy(held[a].at[part], results[a].at[part], sems.at[1, i])
        )
        inward[-1].start()
    for first, second in zip(inward, outward):
        first.wait()
        second.start()
    for second in outward:
        second.wait()


def per_device(
    dims,
    tokens, norm_gain, qkv_codes, qkv_scales, out_codes, out_scales, block_mask, key_counts, upstream,
):
    ZH, Y, ZL, X = dims
    H = Y // 2
    NOWN = ZL * X
    T, D = tokens.shape
    W = 2 * HEAD
    vmem = pl.BlockSpec(memory_space=pltpu.VMEM)
    far = pl.BlockSpec(memory_space=pltpu.HBM)
    buffers = [
        ((T, D), BF),
        ((T, D), BF),
        ((9, T), F32),
        ((T, D), BF),
        ((ZH, Y, 2, ROWS, T), BF),
        ((ZH, Y, 2, ROWS, T), BF),
        ((ZH, Y, ROWS, T), BF),
        ((ZH, Y, ROWS, T), BF),
        ((2, ZH, Y, 2, ROWS, W), BF),
        ((ZH, Y, 2, ROWS, NOWN * HEAD), BF),
        ((2, T, HEAD), BF),
        ((3, 2, T, HEAD), BF),
        ((3, T, T), F32),
        ((3, T, T), BF),
        ((3, T, T), BF),
        ((T, HEAD), BF),
        ((T, NOWN * HEAD), BF),
        ((T, D), BF),
        ((2, 2, T, HEAD), BF),
        ((2, 2, T, HEAD), BF),
        ((2, T, HEAD), F32),
        ((2, T, COLS), BF),
        ((2, Y, ZH, ROWS, W), F32),
        ((2, 2, H, 2, ZH // 2, ROWS, W), BF),
        ((2, 2, H, 2, ZH // 2, ROWS, W), BF),
        ((2, ZH, ROWS, W), F32),
        ((2, ZH, ROWS, W), BF),
        ((2, ZH, ROWS, W), BF),
    ]
    sems = [
        (2, 2, ZH), (2, 2, H, 2, 2), (2, 2, Y), (2, 2, 2), (2, 2), (2, NOWN), (2, NOWN), (2, NOWN),
        (2, 2, 2), (2, 3), (2, 2, 2, H, 2), (2, 2, ZH), (4 + ZH,),
    ]
    mixed, gq, go = pl.pallas_call(
        functools.partial(kernel, dims),
        out_shape=(
            jax.ShapeDtypeStruct((T, D), BF),
            jax.ShapeDtypeStruct((3, ROWS, HEAD), F32),
            jax.ShapeDtypeStruct((ROWS, HEAD), F32),
        ),
        in_specs=[far] + [vmem] * 7 + [far],
        out_specs=(far, vmem, vmem),
        scratch_shapes=[pltpu.VMEM(s, t) for s, t in buffers]
        + [pltpu.SemaphoreType.DMA(s) for s in sems],
        compiler_params=pltpu.CompilerParams(
            collective_id=0, has_side_effects=True, vmem_limit_bytes=63 * 1024 * 1024
        ),
        cost_estimate=pl.CostEstimate(
            flops=4_000_000_000, bytes_accessed=6_000_000, transcendentals=500_000
        ),
    )(
        tokens,
        norm_gain.reshape(1, D),
        qkv_codes.transpose(1, 0, 2),
        qkv_scales.transpose(1, 2, 0),
        out_codes,
        out_scales.transpose(1, 0),
        block_mask,
        key_counts.reshape(1, -1),
        upstream,
    )
    mixed, gq, go = pl.pallas_call(
        store,
        out_shape=tuple(jax.ShapeDtypeStruct(a.shape, a.dtype) for a in (mixed, gq, go)),
        in_specs=[far] * 3,
        out_specs=(far,) * 3,
        scratch_shapes=[pltpu.VMEM(a.shape, a.dtype) for a in (mixed, gq, go)]
        + [pltpu.SemaphoreType.DMA((2, 6))],
        compiler_params=pltpu.CompilerParams(vmem_limit_bytes=63 * 1024 * 1024),
    )(mixed, gq, go)
    return mixed, gq.transpose(1, 0, 2), go


def build(torus):
    s = torus.shape
    dims = (s["zh"], s["y"], s["zl"], s["x"])
    placed = (
        P(DP, None), P(), P(DP, None, OWN), P(DP, None, OWN), P(DP, OWN), P(DP, OWN), P(DP, None),
        P(), P(DP, None),
    )
    return jax.shard_map(
        functools.partial(per_device, dims),
        mesh=torus,
        in_specs=placed,
        out_specs=(P(DP, None), P(DP, None, OWN), P(DP, OWN)),
        check_vma=False,
    )


def solution(mesh):
    return build(Mesh(mesh.devices.reshape(4, 8, 2, 2, 4), AXES))
```

```python
import functools
import math

import jax
import jax.numpy as jnp
from jax import lax
from jax.experimental import pallas as pl
from jax.experimental.pallas import tpu as pltpu
from jax.sharding import Mesh
from jax.sharding import PartitionSpec as P

HEAD = 128
BLK = 128
ROWS = 32
COLS = 4 * HEAD
AXES = ("zh", "y", "core", "zl", "x")
DP = ("zh", "y", "core")
OWN = ("zl", "x")
BF = jnp.bfloat16
F32 = jnp.float32
MESH = pl.DeviceIdType.MESH
INV_ROOT = 1.0 / HEAD**0.5
TO_EXP2 = INV_ROOT * math.log2(math.e)


def nn(a, b):
    return lax.dot_general(a, b, (((1,), (0,)), ((), ())), preferred_element_type=F32)


def nt(a, b):
    return lax.dot_general(a, b, (((1,), (1,)), ((), ())), preferred_element_type=F32)


def tn(a, b):
    return lax.dot_general(a, b, (((0,), (0,)), ((), ())), preferred_element_type=F32)


def kernel(
    dims,
    tok_hbm, gain, codes, scales, ocodes, oscales, maskb, counts, ups_hbm,
    mixed, gq, go,
    tok, ups, bias, normed, ntr, utr, nts, uts, wbuf, wof, qd, kv, ebuf, pbuf, dsb, atts,
    att_all, mixv, hgs, hgr, ogr, dd, g, rss, rsr, fin, zs, zr,
    agz, agy, ags, halo, tsw, wos, wps, ats, hgm, dds, rsm, zsm, loc,
):
    ZH, Y, ZL, X = dims
    H = Y // 2
    ZP = ZH // 2
    W = 2 * HEAD
    NOWN = ZL * X
    T, D = tok.shape
    NQ = T // BLK
    SEG = T // BLK
    zh, y, c = lax.axis_index("zh"), lax.axis_index("y"), lax.axis_index("core")
    own = lax.axis_index("zl") * X + lax.axis_index("x")
    sib = {"core": 1 - c}
    pending = {}
    locals_ = []

    def rcopy(src, dst, sems, index, dev):
        return pltpu.make_async_remote_copy(
            src_ref=src,
            dst_ref=dst,
            send_sem=sems.at[(0, *index)],
            recv_sem=sems.at[(1, *index)],
            device_id=dev,
            device_id_type=MESH,
        )

    def send(src, dst, sems, index, dev):
        cp = rcopy(src, dst, sems, index, dev)
        cp.start()
        pending[id(sems), index] = [cp, True]

    def arrived(dst, sems, index):
        rcopy(dst, dst, sems, index, sib).wait_recv()
        pending[id(sems), index][1] = False

    def finish():
        for cp in locals_:
            cp.wait()
        for cp, due in pending.values():
            if due:
                cp.wait_recv()
            cp.wait_send()

    def keep(src, dst, i):
        cp = pltpu.make_async_copy(src, dst, loc.at[i])
        cp.start()
        return cp

    def zk(k):
        return lax.rem(zh + k, ZH)

    def yd(d):
        return lax.rem(y + (d + Y), Y)

    def ydev(d):
        return {"y": yd(d)}

    def owner(j):
        return lax.rem(own + j, NOWN)

    def odev(o):
        return {"zl": o // X, "x": lax.rem(o, X)}

    def lanes(o, n):
        return pl.ds(pl.multiple_of(o * n, n), n)

    place = (zh * Y + y) * 2 + c
    count = ZH * Y * 2

    def range_dev(step):
        r = lax.rem(place + step + count, count)
        return {"zh": r // (2 * Y), "y": lax.rem(r // 2, Y), "core": lax.rem(r, 2)}

    nxt, prv = range_dev(1), range_dev(-1)

    barrier = pltpu.get_barrier_semaphore()
    partners = [odev(owner(j)) for j in range(1, NOWN)]
    partners += [{"zh": zk(k)} for k in range(1, ZH)]
    partners += [nxt, prv, ydev(2), ydev(-2), ydev(1), ydev(-1)]
    for dev in partners:
        pl.semaphore_signal(barrier, inc=1, device_id=dev, device_id_type=MESH)
    load_tok = keep(tok_hbm, tok, 0)
    load_ups = keep(ups_hbm, ups, 1)

    eye = lax.broadcasted_iota(jnp.int32, (ROWS, ROWS), 0) == lax.broadcasted_iota(
        jnp.int32, (ROWS, ROWS), 1
    )

    def column(row):
        return jnp.sum(jnp.where(eye, row, 0.0), axis=1, keepdims=True)

    for at, j in enumerate((1, 2, 0)):
        part = codes[j].astype(F32) * column(scales[j])
        lo = (at % 2) * HEAD
        wbuf[at // 2, zh, y, c, :, lo : lo + HEAD] = part.astype(BF)
    part = ocodes[...].astype(F32) * column(oscales[...])
    wbuf[1, zh, y, c, :, HEAD:] = part.astype(BF)

    blocks = lax.broadcasted_iota(jnp.int32, counts.shape, 1)
    within = lax.broadcasted_iota(jnp.int32, (1, BLK), 1)
    for j in range(3 * SEG):
        which = place * SEG + (j - SEG)
        alive = jnp.sum(jnp.where(blocks == which, counts[...], 0), axis=1, keepdims=True)
        for b in range(NQ):
            ok = jnp.logical_and(within < alive, maskb[b : b + 1, j : j + 1] > 0)
            row = b * 3 + j // SEG
            lo = (j % SEG) * BLK
            bias[row : row + 1, lo : lo + BLK] = jnp.where(ok, 0.0, -1e30)
    pl.semaphore_wait(barrier, len(partners))

    def piece(h, q, d):
        return wbuf.at[h, pl.ds(q * ZP, ZP), yd(d), c]

    def ag_send(d, t, h, q):
        s = 1 if d == 0 else -1
        b = piece(h, q, -s * (t - 1))
        send(b, b, agy, (d, t - 1, h, q), ydev(s))

    def ag_skip(d, h, q):
        s = 1 if d == 0 else -1
        b = piece(h, q, -s * (H - 2))
        send(b, b, agy, (d, H - 1, h, q), ydev(2 * s))

    def ag_wait(d, t, h, q):
        s = 1 if d == 0 else -1
        arrived(piece(h, q, -s * t), agy, (d, t - 1, h, q))

    def ag_pass(h, dy):
        b = wbuf.at[h, :, yd(dy), c]
        send(b, b, ags, (h, dy % Y), sib)

    def wof_send(dy):
        src = wbuf.at[1, :, yd(dy), c, :, pl.ds(HEAD, HEAD)]
        for j in range(1, NOWN):
            o = owner(j)
            rcopy(src, wof.at[:, yd(dy), c, :, lanes(own, HEAD)], wos, (j,), odev(o)).start()

    def ag_z(h):
        for k in range(1, ZH):
            arrived(wbuf.at[h, zk(ZH - k), y, c], agz, (h, k))
        for q in range(2):
            for d in range(2):
                ag_send(d, 1, h, q)
        ag_pass(h, 0)

    for h in range(2):
        mine = wbuf.at[h, zh, y, c]
        for k in (2, 1, 3)[: ZH - 1] if ZH == 4 else range(1, ZH):
            send(mine, mine, agz, (h, k), {"zh": zk(k)})

    def norm_rows(i, carry):
        r = pl.ds(pl.multiple_of(i * 16, 16), 16)
        x = tok[r, :].astype(F32)
        factor = lax.rsqrt(jnp.mean(x * x, axis=-1, keepdims=True) + 1e-05)
        normed[r, :] = (x * factor * gain[...]).astype(BF)
        return carry

    def turn(src, dst):
        per = Y // 2

        def body(j, carry):
            v = src[:, pl.ds(pl.multiple_of(j * 128, 128), 128)]
            dst[j // per, pl.ds(2 * lax.rem(j, per), 2)] = v.T.reshape(2, 2, ROWS, T)
            return carry

        return body

    load_tok.wait()
    lax.fori_loop(0, T // 16, norm_rows, 0)
    ag_z(0)
    ag_z(1)
    wof_send(0)
    load_ups.wait()

    def fill(t):
        if t == 1:
            lax.fori_loop(0, D // 128, turn(ups, utr), 0)
            send(utr.at[:, :, 1 - c], uts, tsw, (0,), sib)
        if t == 2:
            lax.fori_loop(0, D // 128, turn(normed, ntr), 0)
            send(ntr.at[:, :, 1 - c], nts, tsw, (1,), sib)

    for t in range(1, H):
        for h in range(2):
            for q in range(2):
                for d in range(2):
                    ag_wait(d, t, h, q)
                    if t < H - 1:
                        ag_send(d, t + 1, h, q)
                    if t == H - 2 and q == d:
                        ag_skip(d, h, q)
            ag_pass(h, -t)
            ag_pass(h, t)
            if t == H - 1:
                for d in range(2):
                    ag_wait(d, H, h, d)
                ag_pass(h, H)
        wof_send(-t)
        wof_send(t)
        if t == H - 1:
            wof_send(H)
        fill(t)

    def from_sibling(h):
        for dy in range(Y):
            arrived(wbuf.at[h, :, yd(dy), 1 - c], ags, (h, dy))

    def project(src, h, lo, n):
        total = None
        for z in range(ZH):
            w = wbuf[h, z, :, :, :, lo : lo + n].reshape(Y * 2 * ROWS, n)
            term = nn(src[:, z * Y * 64 : (z + 1) * Y * 64], w)
            total = term if total is None else total + term
        return total.astype(BF)

    from_sibling(0)
    keyval = project(normed, 0, 0, W)
    kv[1, 0] = keyval[:, :HEAD]
    kv[1, 1] = keyval[:, HEAD:]
    for j in range(2):
        send(kv.at[1, j], kv.at[0, j], halo, (0, j), nxt)
        send(kv.at[1, j], kv.at[2, j], halo, (1, j), prv)
    from_sibling(1)
    qd[0] = project(normed, 1, 0, HEAD)
    qd[1] = project(ups, 1, HEAD, HEAD)
    keep_wo = keep(
        wbuf.at[1, :, :, :, :, pl.ds(HEAD, HEAD)], wof.at[:, :, :, :, lanes(own, HEAD)], 2
    )

    sums = [None] * NQ
    for seg in (1, 0, 2):
        if seg != 1:
            arrived(kv.at[seg, 0], halo, (seg // 2, 0))
        for b in range(NQ):
            rows = slice(b * BLK, (b + 1) * BLK)
            score = nt(qd[0, rows, :], kv[seg, 0])
            e = jnp.exp2(score * TO_EXP2 + bias[b * 3 + seg : b * 3 + seg + 1, :])
            ebuf[seg, rows, :] = e
            part = jnp.sum(e, axis=-1, keepdims=True)
            sums[b] = part if sums[b] is None else sums[b] + part
    for seg in (0, 2):
        arrived(kv.at[seg, 1], halo, (seg // 2, 1))
    deltas = []
    for b in range(NQ):
        rows = slice(b * BLK, (b + 1) * BLK)
        scale = 1.0 / sums[b]
        total = None
        for seg in range(3):
            p = ebuf[seg, rows, :] * scale
            ebuf[seg, rows, :] = p
            pb = p.astype(BF)
            pbuf[seg, rows, :] = pb
            term = nn(pb, kv[seg, 1])
            total = term if total is None else total + term
        atts[rows, :] = total.astype(BF)
        deltas.append(jnp.sum(total * qd[1, rows, :].astype(F32), axis=-1, keepdims=True))
    dd[0, :, 3 * HEAD :] = atts[...]
    send(dd.at[0, :, pl.ds(3 * HEAD, HEAD)], dd.at[1, :, pl.ds(3 * HEAD, HEAD)], dds, (0,), sib)

    def to_neighbour(seg, j, value):
        side = seg // 2
        hgs[side, j] = value.astype(BF)
        send(hgs.at[side, j], hgr.at[side, j], hgm, (side, j), prv if seg == 0 else nxt)

    for seg in (0, 2):
        to_neighbour(seg, 1, tn(pbuf[seg], qd[1]))
    for j in range(1, NOWN):
        send(atts, att_all.at[:, lanes(own, HEAD)], ats, (j,), odev(owner(j)))
    keep_att = keep(atts, att_all.at[:, lanes(own, HEAD)], 3)
    for seg in (0, 2, 1):
        for b in range(NQ):
            rows = slice(b * BLK, (b + 1) * BLK)
            dp = nt(qd[1, rows, :], kv[seg, 1])
            dsb[seg, rows, :] = (ebuf[seg, rows, :] * (dp - deltas[b]) * INV_ROOT).astype(BF)
        if seg != 1:
            to_neighbour(seg, 0, tn(dsb[seg], qd[0]))
    for b in range(NQ):
        rows = slice(b * BLK, (b + 1) * BLK)
        total = nn(dsb[0, rows, :], kv[0, 0])
        for seg in (1, 2):
            total += nn(dsb[seg, rows, :], kv[seg, 0])
        dd[0, rows, W : 3 * HEAD] = total.astype(BF)
    part = pl.ds(W, HEAD)
    send(dd.at[0, :, part], dd.at[1, :, part], dds, (1,), sib)
    ogr[0] = tn(dsb[1], qd[0])
    ogr[1] = tn(pbuf[1], qd[1])

    high = ZH * ROWS

    def pair(own_rows, sib_rows, dy, lo, n):
        yy = yd(dy)
        a = nn(own_rows[:, yy, c].reshape(high, T), dd[0, :, lo : lo + n])
        a += nn(sib_rows[:, yy].reshape(high, T), dd[1, :, lo : lo + n])
        return a.reshape(ZH, ROWS, n)

    def term_at(h, dy):
        if h == 0:
            g[0, dy % Y] = pair(ntr, nts, dy, 0, W)
        else:
            g[1, dy % Y, :, :, :HEAD] = pair(ntr, nts, dy, W, HEAD)
            g[1, dy % Y, :, :, HEAD:] = pair(utr, uts, dy, W + HEAD, HEAD)

    def zrange(q):
        return pl.ds(q * ZP, ZP)

    def rs_terms(h, t):
        for dy in {0: (H, H - 1, 1 - H), 1: (H - 2, 2 - H), 2: (1, -1, 0)}[t]:
            term_at(h, dy)

    def rs_send(val, h, d, t, q, hops):
        rss[h, d, t, q] = val.astype(BF)
        send(rss.at[h, d, t, q], rsr.at[h, d, t, q], rsm, (h, d, t, q), ydev(hops))

    def rs_got(h, d, t, q):
        arrived(rsr.at[h, d, t, q], rsm, (h, d, t, q))
        return rsr[h, d, t, q].astype(F32)

    def rs_step(h, t):
        for q in range(2):
            for d in range(2):
                s = 1 if d == 0 else -1
                far = H - 1 - t
                val = g[h, (s * far) % Y, zrange(q)]
                if t == 0:
                    if q == d:
                        rs_send(g[h, H, zrange(q)], h, d, 0, q, 2 * s)
                else:
                    val += rs_got(h, d, t, q)
                    if t == 1 and q == d:
                        val += rs_got(h, d, 0, q)
                rs_send(val, h, d, t + 1, q, s)

    def rs_last(h):
        for q in range(2):
            val = g[h, 0, zrange(q)]
            for d in range(2):
                arrived(rsr.at[h, d, H - 1, q], rsm, (h, d, H - 1, q))
                val += rsr[h, d, H - 1, q].astype(F32)
            fin[h, zrange(q)] = val
        for k in (2, 1, 3)[: ZH - 1] if ZH == 4 else range(1, ZH):
            zs[h, k] = fin[h, zk(k)].astype(BF)
            send(zs.at[h, k], zr.at[h, k], zsm, (h, k), {"zh": zk(k)})

    def rs_end(h):
        val = fin[h, zh]
        for k in range(1, ZH):
            arrived(zr.at[h, k], zsm, (h, k))
            val += zr[h, k].astype(F32)
        return val

    def wof_part(o, core):
        return wof.at[:, :, core, :, lanes(o, HEAD)]

    def wof_pass():
        for j in range(1, NOWN):
            part = wof_part(owner(NOWN - j), c)
            rcopy(part, part, wos, (j,), sib).wait_recv()
            send(part, part, wps, (j,), sib)

    def mix_wait():
        keep_wo.wait()
        keep_att.wait()
        for j in range(1, NOWN):
            o = owner(NOWN - j)
            arrived(wof_part(o, 1 - c), wps, (j,))
            arrived(att_all.at[:, lanes(o, HEAD)], ats, (j,))

    def mix(z):
        n = D // ZH
        w = wof[z].reshape(n, NOWN * HEAD)
        for b in range(NQ):
            rows = slice(b * BLK, (b + 1) * BLK)
            mixv[rows, z * n : (z + 1) * n] = nt(att_all[rows, :], w).astype(BF)
        part = pl.ds(z * n, n)
        locals_.append(keep(mixv.at[:, part], mixed.at[:, part], 4 + z))

    arrived(uts, tsw, (0,))
    arrived(nts, tsw, (1,))
    arrived(dd.at[1, :, pl.ds(3 * HEAD, HEAD)], dds, (0,))
    arrived(dd.at[1, :, pl.ds(W, HEAD)], dds, (1,))
    rs_terms(1, 0)
    rs_step(1, 0)
    rs_terms(1, 1)
    for side in range(2):
        for j in range(2):
            arrived(hgr.at[side, j], hgm, (side, j))
    for j in range(2):
        both = ogr[j] + hgr[0, j].astype(F32) + hgr[1, j].astype(F32)
        dd[0, :, j * HEAD : (j + 1) * HEAD] = both.astype(BF)
    send(dd.at[0, :, pl.ds(0, W)], dd.at[1, :, pl.ds(0, W)], dds, (2,), sib)
    rs_step(1, 1)
    rs_terms(1, 2)
    arrived(dd.at[1, :, pl.ds(0, W)], dds, (2,))
    rs_terms(0, 0)
    rs_step(0, 0)
    rs_terms(0, 1)
    rs_step(1, 2)
    rs_terms(0, 2)
    rs_step(0, 1)
    wof_pass()
    rs_last(1)
    rs_step(0, 2)
    mix_wait()
    for z in range(ZH // 2):
        mix(z)
    rs_last(0)
    for z in range(ZH // 2, ZH):
        mix(z)
    early = rs_end(1)
    gq[0] = early[:, :HEAD]
    go[...] = early[:, HEAD:]
    late = rs_end(0)
    gq[1] = late[:, :HEAD]
    gq[2] = late[:, HEAD:]
    part = wbuf.at[1, :, :, c, :, pl.ds(HEAD, HEAD)]
    for j in range(1, NOWN):
        rcopy(part, wof_part(own, c), wos, (j,), odev(owner(j))).wait_send()
    finish()


def store(*refs):
    sources, results, held, sems = refs[:3], refs[3:6], refs[6:9], refs[9]
    rows = sources[0].shape[0] // 4
    parts = [(0, pl.ds(i * rows, rows)) for i in range(4)] + [(1, slice(None)), (2, slice(None))]
    inward, outward = [], []
    for i, (a, part) in enumerate(parts):
        inward.append(
            pltpu.make_async_copy(sources[a].at[part], held[a].at[part], sems.at[0, i])
        )
        outward.append(
            pltpu.make_async_copy(held[a].at[part], results[a].at[part], sems.at[1, i])
        )
        inward[-1].start()
    for first, second in zip(inward, outward):
        first.wait()
        second.start()
    for second in outward:
        second.wait()


def per_device(
    dims,
    tokens, norm_gain, qkv_codes, qkv_scales, out_codes, out_scales, block_mask, key_counts, upstream,
):
    ZH, Y, ZL, X = dims
    H = Y // 2
    NOWN = ZL * X
    T, D = tokens.shape
    W = 2 * HEAD
    vmem = pl.BlockSpec(memory_space=pltpu.VMEM)
    far = pl.BlockSpec(memory_space=pltpu.HBM)
    buffers = [
        ((T, D), BF),
        ((T, D), BF),
        ((9, T), F32),
        ((T, D), BF),
        ((ZH, Y, 2, ROWS, T), BF),
        ((ZH, Y, 2, ROWS, T), BF),
        ((ZH, Y, ROWS, T), BF),
        ((ZH, Y, ROWS, T), BF),
        ((2, ZH, Y, 2, ROWS, W), BF),
        ((ZH, Y, 2, ROWS, NOWN * HEAD), BF),
        ((2, T, HEAD), BF),
        ((3, 2, T, HEAD), BF),
        ((3, T, T), F32),
        ((3, T, T), BF),
        ((3, T, T), BF),
        ((T, HEAD), BF),
        ((T, NOWN * HEAD), BF),
        ((T, D), BF),
        ((2, 2, T, HEAD), BF),
        ((2, 2, T, HEAD), BF),
        ((2, T, HEAD), F32),
        ((2, T, COLS), BF),
        ((2, Y, ZH, ROWS, W), F32),
        ((2, 2, H, 2, ZH // 2, ROWS, W), BF),
        ((2, 2, H, 2, ZH // 2, ROWS, W), BF),
        ((2, ZH, ROWS, W), F32),
        ((2, ZH, ROWS, W), BF),
        ((2, ZH, ROWS, W), BF),
    ]
    sems = [
        (2, 2, ZH), (2, 2, H, 2, 2), (2, 2, Y), (2, 2, 2), (2, 2), (2, NOWN), (2, NOWN), (2, NOWN),
        (2, 2, 2), (2, 3), (2, 2, 2, H, 2), (2, 2, ZH), (4 + ZH,),
    ]
    mixed, gq, go = pl.pallas_call(
        functools.partial(kernel, dims),
        out_shape=(
            jax.ShapeDtypeStruct((T, D), BF),
            jax.ShapeDtypeStruct((3, ROWS, HEAD), F32),
            jax.ShapeDtypeStruct((ROWS, HEAD), F32),
        ),
        in_specs=[far] + [vmem] * 7 + [far],
        out_specs=(far, vmem, vmem),
        scratch_shapes=[pltpu.VMEM(s, t) for s, t in buffers]
        + [pltpu.SemaphoreType.DMA(s) for s in sems],
        compiler_params=pltpu.CompilerParams(
            collective_id=0, has_side_effects=True, vmem_limit_bytes=63 * 1024 * 1024
        ),
        cost_estimate=pl.CostEstimate(
            flops=4_000_000_000, bytes_accessed=6_000_000, transcendentals=500_000
        ),
    )(
        tokens,
        norm_gain.reshape(1, D),
        qkv_codes.transpose(1, 0, 2),
        qkv_scales.transpose(1, 2, 0),
        out_codes,
        out_scales.transpose(1, 0),
        block_mask,
        key_counts.reshape(1, -1),
        upstream,
    )
    mixed, gq, go = pl.pallas_call(
        store,
        out_shape=tuple(jax.ShapeDtypeStruct(a.shape, a.dtype) for a in (mixed, gq, go)),
        in_specs=[far] * 3,
        out_specs=(far,) * 3,
        scratch_shapes=[pltpu.VMEM(a.shape, a.dtype) for a in (mixed, gq, go)]
        + [pltpu.SemaphoreType.DMA((2, 6))],
        compiler_params=pltpu.CompilerParams(vmem_limit_bytes=63 * 1024 * 1024),
    )(mixed, gq, go)
    return mixed, gq.transpose(1, 0, 2), go


def build(torus):
    s = torus.shape
    dims = (s["zh"], s["y"], s["zl"], s["x"])
    placed = (
        P(DP, None), P(), P(DP, None, OWN), P(DP, None, OWN), P(DP, OWN), P(DP, OWN), P(DP, None),
        P(), P(DP, None),
    )
    return jax.shard_map(
        functools.partial(per_device, dims),
        mesh=torus,
        in_specs=placed,
        out_specs=(P(DP, None), P(DP, None, OWN), P(DP, OWN)),
        check_vma=False,
    )


def solution(mesh):
    return build(Mesh(mesh.devices.reshape(4, 8, 2, 2, 4), AXES))
```
